32 devices in a mesh: row: 8 (over z, x), col: 4 (over y, core).
Axes of the slice: x: 2, y: 2, z: 4, core: 2. Of those that a mesh axis runs over, the one named last changes fastest.
Arguments:
- feats: bfloat16 [8, 2, 64, 96], P('row', None, 'col'), may hold values from -6 to 6
- proj_weight: bfloat16 [96, 48], replicated, may hold values from -0.625 to 0.625
- conv_weight: bfloat16 [48, 9, 48], replicated, may hold values from -0.3125 to 0.3125
- head_weight: float32 [48], replicated, may hold values from -0.875 to 0.875
- tile_table: int32 [8, 4, 5, 3], P('row', 'col'), may hold values from 0 to 15, as said below
- targets: float32 [8, 4, 5, 64, 64], P('row', 'col'), may hold values from -10 to 10
Outputs:
- feat_grad: float32 [8, 2, 64, 96], P('row', None, 'col')
- proj_grad: float32 [96, 48], replicated
- conv_grad: float32 [48, 9, 48], replicated
- head_grad: float32 [48], replicated
The draws below stay inside these ranges and needn't reach their ends.
Inputs may be any that keep to these rules, and one draw needn't show every extreme that they name: `tile_table`: for row index r, the slots over all column indices hold every tile (a, b) with a in r, 15 - r and a <= b exactly once as (a, b, 1); every other slot holds (r, r, 0). The tiles of row r then of row 15 - r, by rising column, are dealt one per column index in turn from a column index drawn for each r.
All inputs are finite; a program needn't handle non-finite values.
Results may differ from the reference program's by a relative error of at most 0.0043.
Values may be sent and summed in bfloat16 or wider, within the bound.
No kernel may reach another device: no remote copies, remote signals or barrier semaphores. Data moves between devices by JAX's collectives and lax.ppermute only.
A program may use at most 64 MiB of HBM per device.

```python
import math
import jax
import jax.numpy as jnp
from jax import lax

C1 = 96
MAP_CHANNELS = 48
TILE_BINS = 64
DILATION_SIZE = 8
NB = 16
K = 5
N_ROW = 8
N_COL = 4


def draw_tile_table(key, part):
    shifts = jax.random.randint(key, (N_ROW,), 0, N_COL)
    shape = (N_ROW, N_COL, K)
    band_idx = jnp.broadcast_to(jnp.arange(N_ROW, dtype=jnp.int32)[:, None, None], shape)
    column = jnp.broadcast_to(jnp.arange(N_COL, dtype=jnp.int32)[None, :, None], shape)
    slot_idx = jnp.broadcast_to(jnp.arange(K, dtype=jnp.int32)[None, None, :], shape)
    number = slot_idx * N_COL + (column - shifts[:, None, None]) % N_COL
    first_count = NB - band_idx
    upper = number < first_count
    tile_row_index = jnp.where(upper, band_idx, NB - 1 - band_idx)
    tile_column_index = jnp.where(upper, band_idx + number, NB - 1 - band_idx + (number - first_count))
    is_live = number <= NB
    tile_row_index = jnp.where(is_live, tile_row_index, band_idx)
    tile_column_index = jnp.where(is_live, tile_column_index, band_idx)
    return jnp.stack([tile_row_index, tile_column_index, is_live.astype(jnp.int32)], axis=-1).astype(jnp.int32)


def level_of(rng, dims, pieces, least, high):
    factor_of, own = 1.0, jax.random.fold_in(rng, 6)
    for dim, blocks in pieces:
        draws = jnp.exp(jax.random.uniform(jax.random.fold_in(own, dim), (blocks,), jnp.float32, least / len(pieces), high / len(pieces)))
        factor_of = factor_of * jnp.repeat(draws, dims[dim] // blocks).reshape([-1 if axis == dim else 1 for axis in range(len(dims))])
    return factor_of


def normal_values(own_key, extent, width, reach, split=(), kind=jnp.bfloat16):
    values = jax.random.normal(own_key, extent, jnp.float32) * width
    if len(split) > 0:
        values = level_of(own_key, extent, split, -0.22, 0.18) * values
    return jnp.clip(values, min=-reach, max=reach).astype(kind)


def setup_inputs(seed: int = 0) -> dict:
    keys = jax.random.split(jax.random.key(seed), 7)
    return {
        "feats": normal_values(keys[0], (N_ROW, 2, TILE_BINS, C1), 1.0, 6.0, ((0, 8), (2, 4))),
        "proj_weight": normal_values(keys[1], (C1, MAP_CHANNELS), C1 ** -0.5, 0.625),
        "conv_weight": normal_values(keys[2], (MAP_CHANNELS, 9, MAP_CHANNELS), (9 * MAP_CHANNELS) ** -0.5, 0.3125),
        "head_weight": normal_values(keys[3], (MAP_CHANNELS,), MAP_CHANNELS ** -0.5, 0.875, (), jnp.float32),
        "tile_table": draw_tile_table(jax.random.fold_in(keys[6], 71), 0),
        "targets": normal_values(keys[5], (N_ROW, N_COL, K, TILE_BINS, TILE_BINS), 2.0, 10.0, ((0, 8), (1, 4)), jnp.float32),
    }


def tile_terms(padded_map, conv_flat, head_weight, sequence_length, tile_row_index, tile_column_index, is_live, goal):
    padded_extent = TILE_BINS + 2 * DILATION_SIZE
    rows_part = lax.dynamic_slice_in_dim(padded_map, (tile_row_index * TILE_BINS).astype(jnp.int32), padded_extent, 0)
    cols_part = lax.dynamic_slice_in_dim(padded_map, (tile_column_index * TILE_BINS).astype(jnp.int32), padded_extent, 0)
    step_index = jnp.arange(padded_extent, dtype=jnp.int32)
    row_position = tile_row_index * TILE_BINS - DILATION_SIZE + step_index
    column_position = tile_column_index * TILE_BINS - DILATION_SIZE + step_index
    in_row = (row_position >= 0) & (row_position < sequence_length)
    in_col = (column_position >= 0) & (column_position < sequence_length)
    paired_map = 0.5 * (rows_part.T.astype(jnp.float32)[:, :, None] + cols_part.T.astype(jnp.float32)[:, None, :])
    active = in_row[None, :, None] & in_col[None, None, :] & (paired_map > 0)
    relu_act = jnp.where(active, paired_map, jnp.zeros_like(paired_map)).astype(jnp.bfloat16)
    tap_shifts = [(row_shift, column_shift) for row_shift in (0, DILATION_SIZE, 2 * DILATION_SIZE) for column_shift in (0, DILATION_SIZE, 2 * DILATION_SIZE)]
    stacked = jnp.concatenate([relu_act[:, row_shift:row_shift + TILE_BINS, column_shift:column_shift + TILE_BINS].reshape(MAP_CHANNELS, TILE_BINS * TILE_BINS) for row_shift, column_shift in tap_shifts], axis=0)
    inner_region = paired_map[:, DILATION_SIZE:DILATION_SIZE + TILE_BINS, DILATION_SIZE:DILATION_SIZE + TILE_BINS].reshape(MAP_CHANNELS, TILE_BINS * TILE_BINS)
    outputs = inner_region + jnp.dot(conv_flat, stacked, preferred_element_type=jnp.float32)
    predicted = jnp.dot(head_weight, outputs, precision=lax.Precision.HIGHEST)
    misfit = (predicted - goal.reshape(TILE_BINS * TILE_BINS)) * is_live.astype(jnp.float32)
    output_gradient_whole = head_weight[:, None] * misfit[None, :]
    dy_half = output_gradient_whole.astype(jnp.bfloat16)
    conv_term = lax.dot_general(dy_half, stacked, (((1,), (1,)), ((), ())), preferred_element_type=jnp.float32)
    head_term = jnp.dot(outputs, misfit, precision=lax.Precision.HIGHEST)
    backed = lax.dot_general(conv_flat, dy_half, (((0,), (0,)), ((), ())), preferred_element_type=jnp.float32)
    up_grad = jnp.zeros((MAP_CHANNELS, padded_extent, padded_extent), jnp.float32)
    for index, (row_shift, column_shift) in enumerate(tap_shifts):
        up_grad = up_grad.at[:, row_shift:row_shift + TILE_BINS, column_shift:column_shift + TILE_BINS].add(backed[index * MAP_CHANNELS:(index + 1) * MAP_CHANNELS].reshape(MAP_CHANNELS, TILE_BINS, TILE_BINS))
    input_gradient = jnp.where(active, up_grad, jnp.zeros_like(up_grad))
    input_gradient = input_gradient.at[:, DILATION_SIZE:DILATION_SIZE + TILE_BINS, DILATION_SIZE:DILATION_SIZE + TILE_BINS].add(output_gradient_whole.reshape(MAP_CHANNELS, TILE_BINS, TILE_BINS))
    grad_rows = 0.5 * lax.optimization_barrier(jnp.sum(input_gradient, axis=2)).T
    grad_cols = 0.5 * lax.optimization_barrier(jnp.sum(input_gradient, axis=1)).T
    return (conv_term, head_term, grad_rows, grad_cols)

def reference(feats, proj_weight, conv_weight, head_weight, tile_table, targets):
    block_list = 2 * N_ROW
    sequence_length = block_list * TILE_BINS
    padded_extent = TILE_BINS + 2 * DILATION_SIZE
    natural_order = jnp.concatenate([feats[:, 0], feats[::-1, 1]], axis=0).reshape(sequence_length, C1)
    projected_map = jnp.dot(natural_order, proj_weight, preferred_element_type=jnp.float32).astype(jnp.bfloat16)
    padded_map = jnp.pad(projected_map, ((DILATION_SIZE, DILATION_SIZE), (0, 0)))
    conv_flat = conv_weight.reshape(MAP_CHANNELS, 9 * MAP_CHANNELS)
    table_flat = tile_table.reshape(N_ROW * N_COL, K, 3)
    goals_flat = targets.reshape(N_ROW * N_COL, K, TILE_BINS, TILE_BINS)

    def per_slot(pair):
        entry, goal = pair
        return tile_terms(padded_map, conv_flat, head_weight, sequence_length, entry[0], entry[1], entry[2], goal)

    def device_step(carry, inputs):
        conv_acc, head_acc, scratch_buffer = carry
        entries, goals = inputs
        conv_term, head_term, grad_rows, grad_cols = lax.map(per_slot, (entries, goals))
        step_index = jnp.arange(padded_extent, dtype=jnp.int32)
        idx_rows = entries[:, 0][:, None] * TILE_BINS + step_index[None, :]
        idx_cols = entries[:, 1][:, None] * TILE_BINS + step_index[None, :]
        scratch_buffer = scratch_buffer.at[idx_rows].add(grad_rows)
        scratch_buffer = scratch_buffer.at[idx_cols].add(grad_cols)
        return ((conv_acc + lax.optimization_barrier(jnp.sum(conv_term, axis=0)), head_acc + lax.optimization_barrier(jnp.sum(head_term, axis=0)), scratch_buffer), None)
    initial_carry = (jnp.zeros((MAP_CHANNELS, 9 * MAP_CHANNELS), jnp.float32), jnp.zeros((MAP_CHANNELS,), jnp.float32), jnp.zeros((sequence_length + 2 * DILATION_SIZE, MAP_CHANNELS), jnp.float32))
    (conv_acc, head_acc, scratch_buffer), _ = lax.scan(device_step, initial_carry, (table_flat, goals_flat))
    gate_gradient = scratch_buffer[DILATION_SIZE:DILATION_SIZE + sequence_length]
    scale = 1.0 / (sequence_length * TILE_BINS)
    proj_grad = jnp.dot(natural_order.astype(jnp.float32).T, gate_gradient, precision=lax.Precision.HIGHEST) * scale
    feat_nat = jnp.dot(gate_gradient, proj_weight.astype(jnp.float32).T, precision=lax.Precision.HIGHEST) / math.sqrt(sequence_length)
    feat_nat = feat_nat.reshape(block_list, TILE_BINS, C1)
    feat_grad = jnp.stack([feat_nat[:N_ROW], feat_nat[N_ROW:][::-1]], axis=1)
    conv_grad = (conv_acc * scale).reshape(MAP_CHANNELS, 9, MAP_CHANNELS)
    head_grad = head_acc * scale
    return (feat_grad, proj_grad, conv_grad, head_grad)
```

```python
import functools
import math

import jax
import jax.numpy as jnp
from jax import lax
from jax.experimental import pallas as pl
from jax.experimental.pallas import tpu as pltpu
from jax.sharding import PartitionSpec as P

DIL = 8
LANES = 128
HALO = 16
F32 = jnp.float32
BF16 = jnp.bfloat16
OUTSIDE = -1e30


def lane_iota(rows):
    return lax.broadcasted_iota(jnp.int32, (rows, LANES), 1)


def split_two(x):
    high = x.astype(BF16).astype(F32)
    return high, x - high


def pad_to(x, rows, cols):
    r, c = x.shape
    if c < cols:
        x = jnp.concatenate([x, jnp.zeros((r, cols - c), x.dtype)], axis=1)
    if r < rows:
        x = jnp.concatenate([x, jnp.zeros((rows - r, cols), x.dtype)], axis=0)
    return x


def column_of(scalars_ref, count):
    sub = lax.broadcasted_iota(jnp.int32, (8, LANES), 0)
    groups = []
    for g in range(count // 8):
        acc = jnp.zeros((8, LANES), F32)
        for k in range(8):
            acc = jnp.where(sub == k, scalars_ref[g * 8 + k], acc)
        groups.append(acc)
    return jnp.concatenate(groups, axis=0)


def tiles_kernel(
    rows_dev,
    slots,
    feats_ref,
    proj_ref,
    conv_ref,
    head_ref,
    table_ref,
    targets_ref,
    out_ref,
    fwin_ref,
    gwin_ref,
    dwin_ref,
    u_ref,
    m_ref,
):
    n_src, _, chunk, c1 = feats_ref.shape
    cols_dev = n_src // rows_dev
    blocks = 2 * rows_dev
    bins = cols_dev * chunk
    ch = proj_ref.shape[1]
    frame = bins + 2 * DIL
    lane = lane_iota(ch)
    lane1 = lane_iota(1)

    def chunks_of(b):
        r, half = (b, 0) if b < rows_dev else (blocks - 1 - b, 1)
        return [feats_ref[r * cols_dev + c, half] for c in range(cols_dev)]

    proj_t = jnp.transpose(pad_to(proj_ref[...].astype(F32), LANES, LANES))[:ch, :c1].astype(BF16)
    zero_halo = jnp.zeros((HALO, c1), BF16)
    for b in range(blocks):
        before = chunks_of(b - 1)[-1][chunk - HALO :] if b > 0 else zero_halo
        after = chunks_of(b + 1)[0][:HALO] if b < blocks - 1 else zero_halo
        tail = jnp.zeros((LANES - bins - 2 * HALO, c1), BF16)
        window = jnp.concatenate([before] + chunks_of(b) + [after, tail], axis=0)
        fwin_ref[b] = window
        g = lax.dot_general(proj_t, window, (((1,), (1,)), ((), ())), preferred_element_type=F32)
        g = 0.5 * g.astype(BF16).astype(F32)
        if b == 0:
            g = jnp.where(lane < HALO, OUTSIDE, g)
        if b == blocks - 1:
            g = jnp.where(lane >= HALO + bins, OUTSIDE, g)
        gwin_ref[b] = g
        dwin_ref[b] = jnp.zeros((ch, LANES), F32)

    taps = jnp.zeros((9, ch), F32)
    for o in range(ch):
        taps = taps + head_ref[o] * conv_ref[o].astype(F32)
    taps_hi, taps_lo = split_two(taps)
    forward_rows, backward_rows = [], []
    for dy in range(3):
        hi, lo = taps_hi[3 * dy : 3 * dy + 3], taps_lo[3 * dy : 3 * dy + 3]
        forward_rows.append(
            jnp.concatenate([hi, lo, jnp.zeros((10, ch), F32)], axis=0).astype(BF16)
        )
        backward_rows.append(jnp.concatenate([hi, hi, lo, jnp.zeros((7, ch), F32)], axis=0))
    forward_taps = jnp.concatenate(forward_rows, axis=1)
    backward_taps = jnp.transpose(pad_to(jnp.concatenate(backward_rows, axis=0), LANES, LANES))[
        :ch, :48
    ].astype(BF16)
    head_col = column_of(head_ref, ch)

    group = 8 * LANES
    pad_cols = 2 * group
    m_ref[:, :pad_cols] = jnp.zeros((16, pad_cols), BF16)
    m_ref[:, pad_cols + bins * LANES :] = jnp.zeros((16, pad_cols), BF16)
    row8 = lax.broadcasted_iota(jnp.int32, (8, LANES), 0)
    row16 = lax.broadcasted_iota(jnp.int32, (16, LANES), 0)
    inner = (lane1 >= HALO) & (lane1 < HALO + bins)
    low_row = (row16 >= 3) & (row16 < 6)

    def slot(s, carry):
        v_acc, x_acc = carry
        a, b, live = table_ref[0, 0, s, 0], table_ref[0, 0, s, 1], table_ref[0, 0, s, 2]
        weight = jnp.where(inner, live.astype(F32), 0.0)
        gr, gc = gwin_ref[a], gwin_ref[b]
        for i in range(frame):
            at = HALO - DIL + i
            x = gr[:, at : at + 1] + gc
            u_ref[:, i * LANES : (i + 1) * LANES] = jnp.maximum(x, 0.0).astype(BF16)
        pred_r = jnp.sum(jnp.where(lane < HALO + bins, head_col * gr, 0.0), axis=0, keepdims=True)
        pred_c = jnp.sum(jnp.where(lane < HALO + bins, head_col * gc, 0.0), axis=0, keepdims=True)
        m_rows = jnp.zeros((1, LANES), F32)
        m_cols = jnp.zeros((1, LANES), F32)
        for c in range(bins // 8):
            u3 = jnp.concatenate(
                [u_ref[:, (c + dy) * group : (c + dy + 1) * group] for dy in range(3)], axis=0
            )
            z = jnp.dot(forward_taps, u3, preferred_element_type=F32)[:8]
            goal = targets_ref[0, 0, s, c * 8 : (c + 1) * 8, :]
            goal = jnp.concatenate(
                [jnp.zeros((8, HALO), F32), goal, jnp.zeros((8, LANES - HALO - bins), F32)], axis=1
            )
            for k in range(8):
                i = c * 8 + k
                zi = z[:, k * LANES : (k + 1) * LANES]
                shifted = jnp.where(
                    row8 % 3 == 0,
                    pltpu.roll(zi, DIL, 1),
                    jnp.where(row8 % 3 == 2, pltpu.roll(zi, LANES - DIL, 1), zi),
                )
                conv = jnp.sum(jnp.where(row8 < 6, shifted, 0.0), axis=0, keepdims=True)
                at = HALO + i
                m = (conv + pred_c + pred_r[:, at : at + 1] - goal[k : k + 1]) * weight
                m = jnp.where(inner, m, 0.0)
                m_cols = m_cols + m
                m_rows = jnp.where(lane1 == at, jnp.sum(m, axis=1, keepdims=True), m_rows)
                m8 = jnp.broadcast_to(m, (8, LANES))
                left, right = pltpu.roll(m8, LANES - DIL, 1), pltpu.roll(m8, DIL, 1)
                spread = jnp.where(
                    row16 % 3 == 0,
                    jnp.concatenate([left, left], axis=0),
                    jnp.where(
                        row16 % 3 == 2,
                        jnp.concatenate([right, right], axis=0),
                        jnp.concatenate([m8, m8], axis=0),
                    ),
                )
                hi, lo = split_two(spread)
                m_ref[:, pad_cols + i * LANES : pad_cols + (i + 1) * LANES] = jnp.where(
                    low_row, lo, hi
                ).astype(BF16)
        d_rows = jnp.zeros((ch, LANES), F32)
        d_cols = jnp.zeros((ch, LANES), F32)
        for c in range(frame // 8):
            m3 = jnp.concatenate(
                [m_ref[:, (c + 2 - dy) * group : (c + 3 - dy) * group] for dy in range(3)], axis=0
            )
            u = u_ref[:, c * group : (c + 1) * group]
            v_acc = v_acc + lax.dot_general(
                u, m3, (((1,), (1,)), ((), ())), preferred_element_type=F32
            )
            up = jnp.dot(backward_taps, m3, preferred_element_type=F32)
            grad = jnp.where(u.astype(F32) > 0.0, up, 0.0)
            for k in range(8):
                part = grad[:, k * LANES : (k + 1) * LANES]
                d_cols = d_cols + part
                d_rows = jnp.where(
                    lane == HALO - DIL + c * 8 + k, jnp.sum(part, axis=1, keepdims=True), d_rows
                )
        d_rows = 0.5 * (d_rows + head_col * m_rows)
        d_cols = 0.5 * (d_cols + head_col * m_cols)
        dwin_ref[a] = dwin_ref[a] + d_rows
        dwin_ref[b] = dwin_ref[b] + d_cols
        return v_acc, x_acc + jnp.where(m_rows != 0.0, gr * m_rows, 0.0) + jnp.where(
            m_cols != 0.0, gc * m_cols, 0.0
        )

    v_acc, x_acc = lax.fori_loop(
        0, slots, slot, (jnp.zeros((ch, 48), F32), jnp.zeros((ch, LANES), F32))
    )

    proj_acc = jnp.zeros((2 * ch, c1), F32)
    for b in range(blocks):
        hi, lo = split_two(dwin_ref[b])
        both = jnp.concatenate([hi, lo], axis=0).astype(BF16)
        proj_acc = proj_acc + jnp.dot(both, fwin_ref[b], preferred_element_type=F32)
    proj_acc = pad_to(proj_acc[:ch] + proj_acc[ch:], ch, LANES)

    v_pad = pad_to(v_acc, ch, LANES)
    v_pad = v_pad + pltpu.roll(v_pad, LANES - 3, 1)
    sums = jnp.zeros((ch, LANES), F32)
    for dy in range(3):
        first = 2 * ch + 3 * dy
        moved = pltpu.roll(v_pad, 2 * ch - 13 * dy, 1)
        sums = jnp.where((lane >= first) & (lane < first + 3), moved, sums)
    sums = jnp.where(lane == 2 * ch + 9, jnp.sum(x_acc, axis=1, keepdims=True), sums)
    sums_hi, sums_lo = split_two(sums)
    sums = sums_hi + pltpu.roll(sums_lo, 10, 1)
    shared = [
        jnp.where(lane < 2 * ch, half, sums) for half in (pltpu.roll(proj_acc, ch, 1), proj_acc)
    ]

    def block_gradient(b):
        own = jnp.where((lane >= HALO) & (lane < HALO + bins), dwin_ref[b], 0.0)
        if b > 0:
            before = pltpu.roll(dwin_ref[b - 1], LANES - bins, 1)
            own = own + jnp.where((lane >= HALO) & (lane < HALO + DIL), before, 0.0)
        if b < blocks - 1:
            after = pltpu.roll(dwin_ref[b + 1], bins, 1)
            own = own + jnp.where((lane >= HALO + bins - DIL) & (lane < HALO + bins), after, 0.0)
        return jnp.transpose(pad_to(own, LANES, LANES))[HALO : HALO + bins]

    part = bins // (out_ref.shape[0] // rows_dev)
    lane_part = lane_iota(part)
    for r in range(rows_dev):
        both = (block_gradient(r), block_gradient(blocks - 1 - r))
        for c in range(bins // part):
            dest = r * (bins // part) + c
            base = shared[c % 2]
            for half in range(2):
                rows = slice(half * part, (half + 1) * part)
                piece = jnp.where(
                    lane_part < ch, both[half][c * part : (c + 1) * part], base[rows]
                )
                out_ref[dest, rows] = piece.astype(BF16)
            out_ref[dest, 2 * part :] = base[2 * part :].astype(BF16)


def finish_kernel(
    scale, root, got_ref, proj_ref, conv_ref, head_ref, feat_ref, conv_out_ref, head_out_ref, half_ref
):
    n_src, ch, _ = got_ref.shape
    c1 = proj_ref.shape[0]
    part = feat_ref.shape[2]
    total = got_ref[0].astype(F32)
    for d in range(1, n_src):
        total = total + got_ref[d].astype(F32)
    whole_t = jnp.transpose(pad_to(total, LANES, LANES))
    half_ref[...] = whole_t[ch : 2 * ch, :ch] * scale

    proj_t = jnp.transpose(pad_to(proj_ref[...].astype(F32), LANES, LANES))[:ch, :c1].astype(BF16)
    hi, lo = split_two(total[: 2 * part, :ch])
    feat = jnp.dot(hi.astype(BF16), proj_t, preferred_element_type=F32) + jnp.dot(
        lo.astype(BF16), proj_t, preferred_element_type=F32
    )
    feat = feat * root
    for half in range(2):
        feat_ref[0, half] = feat[half * part : (half + 1) * part]

    sums = whole_t[2 * ch : 2 * ch + 10, :ch] + whole_t[2 * ch + 10 : 2 * ch + 20, :ch]
    v = sums[:9]
    sub = lax.broadcasted_iota(jnp.int32, (8, ch), 0)
    groups = []
    for g in range(ch // 8):
        acc = jnp.zeros((8, ch), F32)
        for k in range(8):
            o = g * 8 + k
            conv_out_ref[o] = v * (head_ref[o] * scale)
            product = jnp.sum(conv_ref[o].astype(F32) * v, axis=0, keepdims=True)
            acc = jnp.where(sub == k, product, acc)
        groups.append(acc)
    products = pad_to(jnp.concatenate(groups, axis=0), LANES, LANES)
    head_sum = jnp.sum(jnp.transpose(products), axis=0, keepdims=True)[:, :ch]
    head_out_ref[...] = (sums[9:10] + head_sum) * scale


def body(feats, proj_weight, conv_weight, head_weight, tile_table, targets):
    rows_dev, cols_dev = lax.axis_size("row"), lax.axis_size("col")
    devices = rows_dev * cols_dev
    _, halves, part, c1 = feats.shape
    ch = proj_weight.shape[1]
    bins = part * cols_dev
    blocks = halves * rows_dev
    sequence_length = blocks * bins
    slots = tile_table.shape[2]
    scale = 1.0 / (sequence_length * bins)
    frame = bins + 2 * DIL

    all_feats = lax.all_to_all(
        jnp.broadcast_to(feats, (devices,) + feats.shape[1:]), ("row", "col"), 0, 0, tiled=True
    )
    if part % 16:
        all_feats = (
            all_feats.reshape(rows_dev, cols_dev, halves, part, c1)
            .transpose(0, 2, 1, 3, 4)
            .reshape(rows_dev, halves, bins, c1)
        )
    vmem = pl.BlockSpec(memory_space=pltpu.VMEM)
    smem = pl.BlockSpec(memory_space=pltpu.SMEM)
    params = pltpu.CompilerParams(vmem_limit_bytes=48 * 1024 * 1024)
    partial = pl.pallas_call(
        functools.partial(tiles_kernel, rows_dev, slots),
        out_shape=jax.ShapeDtypeStruct((devices, ch, LANES), BF16),
        in_specs=[vmem, vmem, vmem, smem, smem, vmem],
        out_specs=vmem,
        scratch_shapes=[
            pltpu.VMEM((blocks, LANES, c1), BF16),
            pltpu.VMEM((blocks, ch, LANES), F32),
            pltpu.VMEM((blocks, ch, LANES), F32),
            pltpu.VMEM((ch, frame * LANES), BF16),
            pltpu.VMEM((16, (bins + 32) * LANES), BF16),
        ],
        compiler_params=params,
        name="tiles",
    )(all_feats, proj_weight, conv_weight, head_weight, tile_table, targets)
    got = lax.all_to_all(partial, ("row", "col"), 0, 0, tiled=True)
    feat_grad, conv_grad, head_grad, mine = pl.pallas_call(
        functools.partial(finish_kernel, scale, 1.0 / math.sqrt(sequence_length)),
        out_shape=(
            jax.ShapeDtypeStruct(feats.shape, F32),
            jax.ShapeDtypeStruct(conv_weight.shape, F32),
            jax.ShapeDtypeStruct((1, ch), F32),
            jax.ShapeDtypeStruct((ch, ch), F32),
        ),
        in_specs=[vmem, vmem, vmem, smem],
        out_specs=(vmem, vmem, vmem, vmem),
        compiler_params=params,
        name="finish",
    )(got, proj_weight, conv_weight, head_weight)
    other = lax.ppermute(mine, "col", [(c, c ^ 1) for c in range(cols_dev)])
    odd = lax.axis_index("col") % 2 == 1
    proj_grad = jnp.concatenate(
        [jnp.where(odd, other, mine), jnp.where(odd, mine, other)], axis=0
    )
    return feat_grad, proj_grad, conv_grad, head_grad.reshape(ch)


def solution(mesh):
    return jax.shard_map(
        body,
        mesh=mesh,
        in_specs=(
            P("row", None, "col", None),
            P(),
            P(),
            P(),
            P("row", "col", None, None),
            P("row", "col", None, None, None),
        ),
        out_specs=(P("row", None, "col", None), P(), P(), P()),
        check_vma=False,
    )
```

```python
import functools
import math

import jax
import jax.numpy as jnp
from jax import lax
from jax.experimental import pallas as pl
from jax.experimental.pallas import tpu as pltpu
from jax.sharding import PartitionSpec as P

DIL = 8
LANES = 128
HALO = 16
F32 = jnp.float32
BF16 = jnp.bfloat16
OUTSIDE = -1e30


def lane_iota(rows):
    return lax.broadcasted_iota(jnp.int32, (rows, LANES), 1)


def split_two(x):
    high = x.astype(BF16).astype(F32)
    return high, x - high


def pad_to(x, rows, cols):
    r, c = x.shape
    if c < cols:
        x = jnp.concatenate([x, jnp.zeros((r, cols - c), x.dtype)], axis=1)
    if r < rows:
        x = jnp.concatenate([x, jnp.zeros((rows - r, cols), x.dtype)], axis=0)
    return x


def column_of(scalars_ref, count):
    sub = lax.broadcasted_iota(jnp.int32, (8, LANES), 0)
    groups = []
    for g in range(count // 8):
        acc = jnp.zeros((8, LANES), F32)
        for k in range(8):
            acc = jnp.where(sub == k, scalars_ref[g * 8 + k], acc)
        groups.append(acc)
    return jnp.concatenate(groups, axis=0)


def tiles_kernel(
    rows_dev,
    slots,
    feats_ref,
    proj_ref,
    conv_ref,
    head_ref,
    table_ref,
    targets_ref,
    out_ref,
    fwin_ref,
    gwin_ref,
    dwin_ref,
    u_ref,
    m_ref,
    v_ref,
    forward_ref,
    backward_ref,
):
    n_src, _, chunk, c1 = feats_ref.shape
    cols_dev = n_src // rows_dev
    blocks = 2 * rows_dev
    bins = cols_dev * chunk
    ch = proj_ref.shape[1]
    lane = lane_iota(ch)
    lane1 = lane_iota(1)

    def chunks_of(b):
        r, half = (b, 0) if b < rows_dev else (blocks - 1 - b, 1)
        return [feats_ref[r * cols_dev + c, half] for c in range(cols_dev)]

    proj_t = jnp.transpose(pad_to(proj_ref[...].astype(F32), LANES, LANES))[:ch, :c1].astype(BF16)
    zero_halo = jnp.zeros((HALO, c1), BF16)
    for b in range(blocks):
        before = chunks_of(b - 1)[-1][chunk - HALO :] if b > 0 else zero_halo
        after = chunks_of(b + 1)[0][:HALO] if b < blocks - 1 else zero_halo
        tail = jnp.zeros((LANES - bins - 2 * HALO, c1), BF16)
        window = jnp.concatenate([before] + chunks_of(b) + [after, tail], axis=0)
        fwin_ref[b] = window
        g = lax.dot_general(proj_t, window, (((1,), (1,)), ((), ())), preferred_element_type=F32)
        g = 0.5 * g.astype(BF16).astype(F32)
        if b == 0:
            g = jnp.where(lane < HALO, OUTSIDE, g)
        if b == blocks - 1:
            g = jnp.where(lane >= HALO + bins, OUTSIDE, g)
        gwin_ref[b] = g
        dwin_ref[b] = jnp.zeros((ch, LANES), F32)

    taps = jnp.zeros((9, ch), F32)
    for o in range(ch):
        taps = taps + head_ref[o] * conv_ref[o].astype(F32)
    wide = (8, 8 * ch)
    diagonal = lax.broadcasted_iota(jnp.int32, wide, 1) // ch == lax.broadcasted_iota(
        jnp.int32, wide, 0
    )
    hi_tiles, lo_tiles = [
        [
            jnp.where(diagonal, jnp.broadcast_to(row, wide), 0.0)
            for row in jnp.split(jnp.concatenate([values] * 8, axis=1), 9, axis=0)
        ]
        for values in split_two(taps)
    ]
    forward_rows, backward_rows = [], []
    for dy in range(3):
        hi, lo = hi_tiles[3 * dy : 3 * dy + 3], lo_tiles[3 * dy : 3 * dy + 3]
        forward_rows += hi + lo
        backward_rows += hi + hi + lo + [jnp.zeros(wide, F32)]
    forward_taps = jnp.concatenate(forward_rows, axis=0).astype(BF16)
    backward_taps = jnp.transpose(
        jnp.concatenate(backward_rows + [jnp.zeros((16, 8 * ch), F32)], axis=0)
    )[:, :240].astype(BF16)
    forward_ref[...] = forward_taps
    backward_ref[...] = backward_taps
    head_col = column_of(head_ref, ch)

    groups = bins // 8
    m_ref[:, : 2 * LANES] = jnp.zeros((80, 2 * LANES), BF16)
    m_ref[:, (groups + 2) * LANES :] = jnp.zeros((80, 2 * LANES), BF16)
    v_ref[...] = jnp.zeros(v_ref.shape, F32)
    inner = (lane1 >= HALO) & (lane1 < HALO + bins)

    def slot(s, x_acc):
        a, b, live = table_ref[0, 0, s, 0], table_ref[0, 0, s, 1], table_ref[0, 0, s, 2]
        weight = jnp.where(inner, live.astype(F32), 0.0)
        gr, gc = gwin_ref[a], gwin_ref[b]
        for g in range(groups + 2):
            for k in range(8):
                at = HALO - DIL + g * 8 + k
                x = gr[:, at : at + 1] + gc
                u_ref[k * ch : (k + 1) * ch, g * LANES : (g + 1) * LANES] = jnp.maximum(
                    x, 0.0
                ).astype(BF16)
        pred_r = jnp.sum(jnp.where(lane < HALO + bins, head_col * gr, 0.0), axis=0, keepdims=True)
        pred_c = jnp.sum(jnp.where(lane < HALO + bins, head_col * gc, 0.0), axis=0, keepdims=True)
        pred_r = jnp.transpose(jnp.broadcast_to(pred_r, (LANES, LANES)))
        z = jnp.dot(forward_ref[...], u_ref[...], preferred_element_type=F32)
        m_cols = jnp.zeros((8, LANES), F32)
        row_sums = [jnp.zeros((HALO, LANES), F32)]
        for c in range(groups):
            terms = []
            for dx in range(3):
                tiles = [
                    z[
                        48 * dy + 24 * p + 8 * dx : 48 * dy + 24 * p + 8 * dx + 8,
                        (c + dy) * LANES : (c + dy + 1) * LANES,
                    ]
                    for dy in range(3)
                    for p in range(2)
                ]
                while len(tiles) > 1:
                    tiles = [sum(tiles[i : i + 2]) for i in range(0, len(tiles), 2)]
                terms.append(tiles[0])
            conv = pltpu.roll(terms[0], DIL, 1) + terms[1] + pltpu.roll(terms[2], LANES - DIL, 1)
            goal = targets_ref[0, 0, s, c * 8 : (c + 1) * 8, :]
            goal = jnp.concatenate(
                [jnp.zeros((8, HALO), F32), goal, jnp.zeros((8, LANES - HALO - bins), F32)], axis=1
            )
            at = HALO + c * 8
            m = jnp.where(inner, (conv + pred_c + pred_r[at : at + 8] - goal) * weight, 0.0)
            m_cols = m_cols + m
            row_sums.append(jnp.broadcast_to(jnp.sum(m, axis=1, keepdims=True), (8, LANES)))
            his, los = [], []
            for moved in (pltpu.roll(m, LANES - DIL, 1), m, pltpu.roll(m, DIL, 1)):
                hi, lo = split_two(moved)
                his.append(hi)
                los.append(lo)
            m_ref[:, (c + 2) * LANES : (c + 3) * LANES] = jnp.concatenate(
                his + los + his + [jnp.zeros((8, LANES), F32)], axis=0
            ).astype(BF16)
        row_sums.append(jnp.zeros((LANES - HALO - bins, LANES), F32))
        m_rows = jnp.transpose(jnp.concatenate(row_sums, axis=0))[:1]
        m_cols = jnp.sum(m_cols, axis=0, keepdims=True)
        d_rows = jnp.zeros((ch, LANES), F32)
        d_cols = jnp.zeros((ch, LANES), F32)
        frame_cols = (groups + 2) * LANES
        m3 = jnp.concatenate(
            [m_ref[:, (2 - dy) * LANES : (2 - dy) * LANES + frame_cols] for dy in range(3)], axis=0
        )
        v_ref[...] += lax.dot_general(
            u_ref[...], m3, (((1,), (1,)), ((), ())), preferred_element_type=F32
        )
        for g in range(groups + 2):
            cols = slice(g * LANES, (g + 1) * LANES)
            up = jnp.dot(backward_ref[...], m3[:, cols], preferred_element_type=F32)
            grad = jnp.where(u_ref[:, cols].astype(F32) > 0.0, up, 0.0)
            for k in range(8):
                part = grad[k * ch : (k + 1) * ch]
                d_cols = d_cols + part
                d_rows = jnp.where(
                    lane == HALO - DIL + g * 8 + k, jnp.sum(part, axis=1, keepdims=True), d_rows
                )
        d_rows = 0.5 * (d_rows + head_col * m_rows)
        d_cols = 0.5 * (d_cols + head_col * m_cols)
        dwin_ref[a] = dwin_ref[a] + d_rows
        dwin_ref[b] = dwin_ref[b] + d_cols
        return x_acc + jnp.where(m_rows != 0.0, gr * m_rows, 0.0) + jnp.where(
            m_cols != 0.0, gc * m_cols, 0.0
        )

    x_acc = lax.fori_loop(0, slots, slot, jnp.zeros((ch, LANES), F32))

    proj_acc = jnp.zeros((2 * ch, c1), F32)
    for b in range(blocks):
        hi, lo = split_two(dwin_ref[b])
        both = jnp.concatenate([hi, lo], axis=0).astype(BF16)
        proj_acc = proj_acc + jnp.dot(both, fwin_ref[b], preferred_element_type=F32)
    proj_acc = pad_to(proj_acc[:ch] + proj_acc[ch:], ch, LANES)

    wide = lax.broadcasted_iota(jnp.int32, (ch, 240), 1)
    v_sum = jnp.zeros((ch, 240), F32)
    for k in range(8):
        v_sum = v_sum + jnp.where(wide % 8 == k, v_ref[k * ch : (k + 1) * ch], 0.0)
    hi, lo = split_two(v_sum)
    source = lax.broadcasted_iota(jnp.int32, (240, LANES), 0)
    place = 2 * ch + 3 * (source // 80) + source % 80 % 24 // 8
    select = (source % 80 < 48) & (lax.broadcasted_iota(jnp.int32, (240, LANES), 1) == place)
    sums = jnp.dot(
        jnp.concatenate([hi, lo], axis=0).astype(BF16),
        select.astype(F32).astype(BF16),
        preferred_element_type=F32,
    )
    sums = sums[:ch] + sums[ch:]
    sums = jnp.where(lane == 2 * ch + 9, jnp.sum(x_acc, axis=1, keepdims=True), sums)
    sums_hi, sums_lo = split_two(sums)
    sums = sums_hi + pltpu.roll(sums_lo, 10, 1)
    shared = [
        jnp.where(lane < 2 * ch, half, sums) for half in (pltpu.roll(proj_acc, ch, 1), proj_acc)
    ]

    def block_gradient(b):
        own = jnp.where((lane >= HALO) & (lane < HALO + bins), dwin_ref[b], 0.0)
        if b > 0:
            before = pltpu.roll(dwin_ref[b - 1], LANES - bins, 1)
            own = own + jnp.where((lane >= HALO) & (lane < HALO + DIL), before, 0.0)
        if b < blocks - 1:
            after = pltpu.roll(dwin_ref[b + 1], bins, 1)
            own = own + jnp.where((lane >= HALO + bins - DIL) & (lane < HALO + bins), after, 0.0)
        return jnp.transpose(pad_to(own, LANES, LANES))[HALO : HALO + bins]

    part = bins // (out_ref.shape[0] // rows_dev)
    lane_part = lane_iota(part)
    for r in range(rows_dev):
        both = (block_gradient(r), block_gradient(blocks - 1 - r))
        for c in range(bins // part):
            dest = r * (bins // part) + c
            base = shared[c % 2]
            for half in range(2):
                rows = slice(half * part, (half + 1) * part)
                piece = jnp.where(
                    lane_part < ch, both[half][c * part : (c + 1) * part], base[rows]
                )
                out_ref[dest, rows] = piece.astype(BF16)
            out_ref[dest, 2 * part :] = base[2 * part :].astype(BF16)


def finish_kernel(
    scale, root, got_ref, proj_ref, conv_ref, head_ref, feat_ref, conv_out_ref, head_out_ref, half_ref
):
    n_src, ch, _ = got_ref.shape
    c1 = proj_ref.shape[0]
    part = feat_ref.shape[2]
    total = got_ref[0].astype(F32)
    for d in range(1, n_src):
        total = total + got_ref[d].astype(F32)
    whole_t = jnp.transpose(pad_to(total, LANES, LANES))
    half_ref[...] = whole_t[ch : 2 * ch, :ch] * scale

    proj_t = jnp.transpose(pad_to(proj_ref[...].astype(F32), LANES, LANES))[:ch, :c1].astype(BF16)
    hi, lo = split_two(total[: 2 * part, :ch])
    feat = jnp.dot(hi.astype(BF16), proj_t, preferred_element_type=F32) + jnp.dot(
        lo.astype(BF16), proj_t, preferred_element_type=F32
    )
    feat = feat * root
    for half in range(2):
        feat_ref[0, half] = feat[half * part : (half + 1) * part]

    sums = whole_t[2 * ch : 2 * ch + 10, :ch] + whole_t[2 * ch + 10 : 2 * ch + 20, :ch]
    v = sums[:9]
    sub = lax.broadcasted_iota(jnp.int32, (8, ch), 0)
    groups = []
    for g in range(ch // 8):
        acc = jnp.zeros((8, ch), F32)
        for k in range(8):
            o = g * 8 + k
            conv_out_ref[o] = v * (head_ref[o] * scale)
            product = jnp.sum(conv_ref[o].astype(F32) * v, axis=0, keepdims=True)
            acc = jnp.where(sub == k, product, acc)
        groups.append(acc)
    products = pad_to(jnp.concatenate(groups, axis=0), LANES, LANES)
    head_sum = jnp.sum(jnp.transpose(products), axis=0, keepdims=True)[:, :ch]
    head_out_ref[...] = (sums[9:10] + head_sum) * scale


def body(feats, proj_weight, conv_weight, head_weight, tile_table, targets):
    rows_dev, cols_dev = lax.axis_size("row"), lax.axis_size("col")
    devices = rows_dev * cols_dev
    _, halves, part, c1 = feats.shape
    ch = proj_weight.shape[1]
    bins = part * cols_dev
    blocks = halves * rows_dev
    sequence_length = blocks * bins
    slots = tile_table.shape[2]
    scale = 1.0 / (sequence_length * bins)

    all_feats = lax.all_to_all(
        jnp.broadcast_to(feats, (devices,) + feats.shape[1:]), ("row", "col"), 0, 0, tiled=True
    )
    if part % 16:
        all_feats = (
            all_feats.reshape(rows_dev, cols_dev, halves, part, c1)
            .transpose(0, 2, 1, 3, 4)
            .reshape(rows_dev, halves, bins, c1)
        )
    vmem = pl.BlockSpec(memory_space=pltpu.VMEM)
    smem = pl.BlockSpec(memory_space=pltpu.SMEM)
    params = pltpu.CompilerParams(vmem_limit_bytes=48 * 1024 * 1024)
    partial = pl.pallas_call(
        functools.partial(tiles_kernel, rows_dev, slots),
        out_shape=jax.ShapeDtypeStruct((devices, ch, LANES), BF16),
        in_specs=[vmem, vmem, vmem, smem, smem, vmem],
        out_specs=vmem,
        scratch_shapes=[
            pltpu.VMEM((blocks, LANES, c1), BF16),
            pltpu.VMEM((blocks, ch, LANES), F32),
            pltpu.VMEM((blocks, ch, LANES), F32),
            pltpu.VMEM((8 * ch, (bins // 8 + 2) * LANES), BF16),
            pltpu.VMEM((80, (bins // 8 + 4) * LANES), BF16),
            pltpu.VMEM((8 * ch, 240), F32),
            pltpu.VMEM((144, 8 * ch), BF16),
            pltpu.VMEM((8 * ch, 240), BF16),
        ],
        compiler_params=params,
        name="tiles",
    )(all_feats, proj_weight, conv_weight, head_weight, tile_table, targets)
    got = lax.all_to_all(partial, ("row", "col"), 0, 0, tiled=True)
    feat_grad, conv_grad, head_grad, mine = pl.pallas_call(
        functools.partial(finish_kernel, scale, 1.0 / math.sqrt(sequence_length)),
        out_shape=(
            jax.ShapeDtypeStruct(feats.shape, F32),
            jax.ShapeDtypeStruct(conv_weight.shape, F32),
            jax.ShapeDtypeStruct((1, ch), F32),
            jax.ShapeDtypeStruct((ch, ch), F32),
        ),
        in_specs=[vmem, vmem, vmem, smem],
        out_specs=(vmem, vmem, vmem, vmem),
        compiler_params=params,
        name="finish",
    )(got, proj_weight, conv_weight, head_weight)
    other = lax.ppermute(mine, "col", [(c, c ^ 1) for c in range(cols_dev)])
    odd = lax.axis_index("col") % 2 == 1
    proj_grad = jnp.concatenate(
        [jnp.where(odd, other, mine), jnp.where(odd, mine, other)], axis=0
    )
    return feat_grad, proj_grad, conv_grad, head_grad.reshape(ch)


def solution(mesh):
    return jax.shard_map(
        body,
        mesh=mesh,
        in_specs=(
            P("row", None, "col", None),
            P(),
            P(),
            P(),
            P("row", "col", None, None),
            P("row", "col", None, None, None),
        ),
        out_specs=(P("row", None, "col", None), P(), P(), P()),
        check_vma=False,
    )
```

```python
import functools
import math

import jax
import jax.numpy as jnp
from jax import lax
from jax.experimental import pallas as pl
from jax.experimental.pallas import tpu as pltpu
from jax.sharding import PartitionSpec as P

DIL = 8
LANES = 128
HALO = 16
F32 = jnp.float32
BF16 = jnp.bfloat16
OUTSIDE = -1e30


def lane_iota(rows):
    return lax.broadcasted_iota(jnp.int32, (rows, LANES), 1)


def split_two(x):
    high = x.astype(BF16).astype(F32)
    return high, x - high


def pad_to(x, rows, cols):
    r, c = x.shape
    if c < cols:
        x = jnp.concatenate([x, jnp.zeros((r, cols - c), x.dtype)], axis=1)
    if r < rows:
        x = jnp.concatenate([x, jnp.zeros((rows - r, cols), x.dtype)], axis=0)
    return x


def column_of(scalars_ref, count):
    sub = lax.broadcasted_iota(jnp.int32, (8, LANES), 0)
    groups = []
    for g in range(count // 8):
        acc = jnp.zeros((8, LANES), F32)
        for k in range(8):
            acc = jnp.where(sub == k, scalars_ref[g * 8 + k], acc)
        groups.append(acc)
    return jnp.concatenate(groups, axis=0)


def taps_kernel(conv_ref, head_ref, table_ref, forward_ref, backward_ref, entries_ref):
    ch = conv_ref.shape[1]
    for s in range(table_ref.shape[3]):
        for k in range(3):
            entries_ref[k, s] = table_ref[0, k, 0, s]
    head_col = column_of(head_ref, ch)
    taps = [
        jnp.sum(head_col[:, :ch] * conv_ref[t].astype(F32), axis=0, keepdims=True)
        for t in range(9)
    ]
    wide = (8, 8 * ch)
    diagonal = lax.broadcasted_iota(jnp.int32, wide, 1) // ch == lax.broadcasted_iota(
        jnp.int32, wide, 0
    )
    hi_tiles, lo_tiles = [
        [
            jnp.where(diagonal, jnp.broadcast_to(jnp.concatenate([row] * 8, axis=1), wide), 0.0)
            for row in rows
        ]
        for rows in zip(*[split_two(row) for row in taps])
    ]
    forward_rows, backward_rows = [], []
    for dy in range(3):
        hi, lo = hi_tiles[3 * dy : 3 * dy + 3], lo_tiles[3 * dy : 3 * dy + 3]
        forward_rows += hi + lo
        backward_rows += hi + hi + lo + [jnp.zeros(wide, F32)]
    forward_taps = jnp.concatenate(forward_rows, axis=0).astype(BF16)
    backward_taps = jnp.transpose(
        jnp.concatenate(backward_rows + [jnp.zeros((16, 8 * ch), F32)], axis=0)
    )[:, :240].astype(BF16)
    forward_ref[...] = forward_taps
    backward_ref[...] = backward_taps


def tiles_kernel(
    rows_dev,
    slots,
    feats_ref,
    proj_ref,
    forward_ref,
    backward_ref,
    head_ref,
    table_ref,
    targets_ref,
    out_ref,
    fwin_ref,
    gwin_ref,
    dwin_ref,
    u_ref,
    m_ref,
    v_ref,
):
    n_src, _, chunk, c1 = feats_ref.shape
    cols_dev = n_src // rows_dev
    blocks = 2 * rows_dev
    bins = cols_dev * chunk
    ch = proj_ref.shape[0]
    lane = lane_iota(ch)
    lane1 = lane_iota(1)

    def chunks_of(b):
        r, half = (b, 0) if b < rows_dev else (blocks - 1 - b, 1)
        return [feats_ref[r * cols_dev + c, half] for c in range(cols_dev)]

    zero_halo = jnp.zeros((HALO, c1), BF16)
    for b in range(blocks):
        before = chunks_of(b - 1)[-1][chunk - HALO :] if b > 0 else zero_halo
        after = chunks_of(b + 1)[0][:HALO] if b < blocks - 1 else zero_halo
        tail = jnp.zeros((LANES - bins - 2 * HALO, c1), BF16)
        window = jnp.concatenate([before] + chunks_of(b) + [after, tail], axis=0)
        fwin_ref[b] = window
        g = lax.dot_general(proj_ref[...], window, (((1,), (1,)), ((), ())), preferred_element_type=F32)
        g = 0.5 * g.astype(BF16).astype(F32)
        if b == 0:
            g = jnp.where(lane < HALO, OUTSIDE, g)
        if b == blocks - 1:
            g = jnp.where(lane >= HALO + bins, OUTSIDE, g)
        gwin_ref[b] = g.astype(BF16)
        dwin_ref[b] = jnp.zeros((ch, LANES), F32)

    head_col = column_of(head_ref, ch)
    groups = bins // 8
    m_ref[:, : 2 * LANES] = jnp.zeros((80, 2 * LANES), BF16)
    m_ref[:, (groups + 2) * LANES :] = jnp.zeros((80, 2 * LANES), BF16)
    v_ref[...] = jnp.zeros(v_ref.shape, F32)
    inner = (lane1 >= HALO) & (lane1 < HALO + bins)

    def slot(s, x_acc):
        a, b, live = table_ref[0, s], table_ref[1, s], table_ref[2, s]
        weight = jnp.where(inner, live.astype(F32), 0.0)
        gr, gc = gwin_ref[a].astype(F32), gwin_ref[b].astype(F32)
        pred_r = jnp.sum(jnp.where(lane < HALO + bins, head_col * gr, 0.0), axis=0, keepdims=True)
        pred_c = jnp.sum(jnp.where(lane < HALO + bins, head_col * gc, 0.0), axis=0, keepdims=True)
        pred_r = jnp.transpose(jnp.broadcast_to(pred_r, (LANES, LANES)))

        def activations(g):
            for k in range(8):
                at = HALO - DIL + g * 8 + k
                x = gr[:, at : at + 1] + gc
                u_ref[k * ch : (k + 1) * ch, g * LANES : (g + 1) * LANES] = jnp.maximum(
                    x, 0.0
                ).astype(BF16)
            return jnp.dot(
                forward_ref[...],
                u_ref[:, g * LANES : (g + 1) * LANES],
                preferred_element_type=F32,
            )

        def misfit(c, z):
            terms = []
            for dx in range(3):
                tiles = [
                    z[c + dy][48 * dy + 24 * p + 8 * dx : 48 * dy + 24 * p + 8 * dx + 8]
                    for dy in range(3)
                    for p in range(2)
                ]
                while len(tiles) > 1:
                    tiles = [sum(tiles[i : i + 2]) for i in range(0, len(tiles), 2)]
                terms.append(tiles[0])
            conv = pltpu.roll(terms[0], DIL, 1) + terms[1] + pltpu.roll(terms[2], LANES - DIL, 1)
            goal = targets_ref[0, 0, s, c * 8 : (c + 1) * 8, :]
            goal = jnp.concatenate(
                [jnp.zeros((8, HALO), F32), goal, jnp.zeros((8, LANES - HALO - bins), F32)], axis=1
            )
            at = HALO + c * 8
            m = jnp.where(inner, (conv + pred_c + pred_r[at : at + 8] - goal) * weight, 0.0)
            his, los = [], []
            for moved in (pltpu.roll(m, LANES - DIL, 1), m, pltpu.roll(m, DIL, 1)):
                hi, lo = split_two(moved)
                his.append(hi)
                los.append(lo)
            m_ref[:, (c + 2) * LANES : (c + 3) * LANES] = jnp.concatenate(
                his + los + his + [jnp.zeros((8, LANES), F32)], axis=0
            ).astype(BF16)
            return m

        def gradients(g, d_rows, d_cols):
            cols = slice(g * LANES, (g + 1) * LANES)
            m3 = jnp.concatenate(
                [m_ref[:, (g + 2 - dy) * LANES : (g + 3 - dy) * LANES] for dy in range(3)], axis=0
            )
            up = jnp.dot(backward_ref[...], m3, preferred_element_type=F32)
            grad = jnp.where(u_ref[:, cols].astype(F32) > 0.0, up, 0.0)
            for k in range(8):
                part = grad[k * ch : (k + 1) * ch]
                d_cols = d_cols + part
                d_rows = jnp.where(
                    lane == HALO - DIL + g * 8 + k, jnp.sum(part, axis=1, keepdims=True), d_rows
                )
            return d_rows, d_cols

        z, m_cols, row_sums = [], jnp.zeros((8, LANES), F32), [jnp.zeros((HALO, LANES), F32)]
        d_rows = d_cols = jnp.zeros((ch, LANES), F32)
        for g in range(groups + 2):
            z.append(activations(g))
            if g >= 2:
                m = misfit(g - 2, z)
                m_cols = m_cols + m
                row_sums.append(jnp.broadcast_to(jnp.sum(m, axis=1, keepdims=True), (8, LANES)))
        for g in range(groups + 2):
            d_rows, d_cols = gradients(g, d_rows, d_cols)
        row_sums.append(jnp.zeros((LANES - HALO - bins, LANES), F32))
        m_rows = jnp.transpose(jnp.concatenate(row_sums, axis=0))[:1]
        m_cols = jnp.sum(m_cols, axis=0, keepdims=True)
        frame_cols = (groups + 2) * LANES
        m3 = jnp.concatenate(
            [m_ref[:, (2 - dy) * LANES : (2 - dy) * LANES + frame_cols] for dy in range(3)], axis=0
        )
        v_ref[...] += lax.dot_general(
            u_ref[...], m3, (((1,), (1,)), ((), ())), preferred_element_type=F32
        )
        d_rows = 0.5 * (d_rows + head_col * m_rows)
        d_cols = 0.5 * (d_cols + head_col * m_cols)
        dwin_ref[a] = dwin_ref[a] + d_rows
        dwin_ref[b] = dwin_ref[b] + d_cols
        return x_acc + jnp.where(m_rows != 0.0, gr * m_rows, 0.0) + jnp.where(
            m_cols != 0.0, gc * m_cols, 0.0
        )

    x_acc = lax.fori_loop(0, slots, slot, jnp.zeros((ch, LANES), F32))

    proj_acc = jnp.zeros((2 * ch, c1), F32)
    for b in range(blocks):
        hi, lo = split_two(dwin_ref[b])
        both = jnp.concatenate([hi, lo], axis=0).astype(BF16)
        proj_acc = proj_acc + jnp.dot(both, fwin_ref[b], preferred_element_type=F32)
    proj_acc = pad_to(proj_acc[:ch] + proj_acc[ch:], ch, LANES)

    wide = lax.broadcasted_iota(jnp.int32, (ch, 240), 1)
    v_sum = jnp.zeros((ch, 240), F32)
    for k in range(8):
        v_sum = v_sum + jnp.where(wide % 8 == k, v_ref[k * ch : (k + 1) * ch], 0.0)
    hi, lo = split_two(v_sum)
    source = lax.broadcasted_iota(jnp.int32, (240, LANES), 0)
    place = 2 * ch + 3 * (source // 80) + source % 80 % 24 // 8
    select = (source % 80 < 48) & (lax.broadcasted_iota(jnp.int32, (240, LANES), 1) == place)
    sums = jnp.dot(
        jnp.concatenate([hi, lo], axis=0).astype(BF16),
        select.astype(F32).astype(BF16),
        preferred_element_type=F32,
    )
    sums = sums[:ch] + sums[ch:]
    sums = jnp.where(lane == 2 * ch + 9, jnp.sum(x_acc, axis=1, keepdims=True), sums)
    sums_hi, sums_lo = split_two(sums)
    sums = sums_hi + pltpu.roll(sums_lo, 10, 1)
    shared = [
        jnp.where(lane < 2 * ch, half, sums) for half in (pltpu.roll(proj_acc, ch, 1), proj_acc)
    ]

    def block_gradient(b):
        own = jnp.where((lane >= HALO) & (lane < HALO + bins), dwin_ref[b], 0.0)
        if b > 0:
            before = pltpu.roll(dwin_ref[b - 1], LANES - bins, 1)
            own = own + jnp.where((lane >= HALO) & (lane < HALO + DIL), before, 0.0)
        if b < blocks - 1:
            after = pltpu.roll(dwin_ref[b + 1], bins, 1)
            own = own + jnp.where((lane >= HALO + bins - DIL) & (lane < HALO + bins), after, 0.0)
        return jnp.transpose(pad_to(own, LANES, LANES))[HALO : HALO + bins]

    part = bins // (out_ref.shape[0] // rows_dev)
    lane_part = lane_iota(part)
    for r in range(rows_dev):
        both = (block_gradient(r), block_gradient(blocks - 1 - r))
        for c in range(bins // part):
            dest = r * (bins // part) + c
            base = shared[c % 2]
            for half in range(2):
                rows = slice(half * part, (half + 1) * part)
                piece = jnp.where(
                    lane_part < ch, both[half][c * part : (c + 1) * part], base[rows]
                )
                out_ref[dest, rows] = piece.astype(BF16)
            out_ref[dest, 2 * part :] = base[2 * part :].astype(BF16)


def finish_kernel(
    scale, root, got_ref, proj_ref, conv_ref, head_ref, feat_ref, conv_out_ref, head_out_ref, half_ref
):
    n_src, ch, _ = got_ref.shape
    part = feat_ref.shape[2]
    total = got_ref[0].astype(F32)
    for d in range(1, n_src):
        total = total + got_ref[d].astype(F32)
    half_ref[...] = total[:, ch : 2 * ch] * scale
    whole_t = jnp.transpose(pad_to(total, LANES, LANES))
    proj_t = proj_ref[...]
    hi, lo = split_two(total[: 2 * part, :ch])
    feat = jnp.dot(hi.astype(BF16), proj_t, preferred_element_type=F32) + jnp.dot(
        lo.astype(BF16), proj_t, preferred_element_type=F32
    )
    feat = feat * root
    for half in range(2):
        feat_ref[0, half] = feat[half * part : (half + 1) * part]

    sums = whole_t[2 * ch : 2 * ch + 10, :ch] + whole_t[2 * ch + 10 : 2 * ch + 20, :ch]
    head_col = column_of(head_ref, ch)[:, :ch] * scale
    products = jnp.zeros((ch, ch), F32)
    for t in range(9):
        v = sums[t : t + 1]
        conv_out_ref[t] = head_col * v
        products = products + conv_ref[t].astype(F32) * v
    head_sum = jnp.sum(jnp.transpose(pad_to(products, LANES, LANES)), axis=0, keepdims=True)[:, :ch]
    head_out_ref[...] = (sums[9:10] + head_sum) * scale


def body(feats, proj_weight, conv_weight, head_weight, tile_table, targets):
    rows_dev, cols_dev = lax.axis_size("row"), lax.axis_size("col")
    devices = rows_dev * cols_dev
    _, halves, part, c1 = feats.shape
    ch = proj_weight.shape[1]
    proj_t, conv_t = proj_weight.T, conv_weight.transpose(1, 0, 2)
    bins = part * cols_dev
    blocks = halves * rows_dev
    sequence_length = blocks * bins
    slots = tile_table.shape[2]
    scale = 1.0 / (sequence_length * bins)

    all_feats = lax.all_to_all(
        jnp.broadcast_to(feats, (devices,) + feats.shape[1:]), ("row", "col"), 0, 0, tiled=True
    )
    if part % 16:
        all_feats = (
            all_feats.reshape(rows_dev, cols_dev, halves, part, c1)
            .transpose(0, 2, 1, 3, 4)
            .reshape(rows_dev, halves, bins, c1)
        )
    vmem = pl.BlockSpec(memory_space=pltpu.VMEM)
    smem = pl.BlockSpec(memory_space=pltpu.SMEM)
    params = pltpu.CompilerParams(vmem_limit_bytes=48 * 1024 * 1024)
    forward, backward, entries = pl.pallas_call(
        taps_kernel,
        out_shape=(
            jax.ShapeDtypeStruct((144, 8 * ch), BF16),
            jax.ShapeDtypeStruct((8 * ch, 240), BF16),
            jax.ShapeDtypeStruct((3, slots), jnp.int32),
        ),
        in_specs=[vmem, smem, smem],
        out_specs=(vmem, vmem, smem),
        compiler_params=params,
        cost_estimate=pl.CostEstimate(flops=10**7, bytes_accessed=10**6, transcendentals=0),
        name="taps",
    )(conv_t, head_weight, tile_table.transpose(0, 3, 1, 2))
    partial = pl.pallas_call(
        functools.partial(tiles_kernel, rows_dev, slots),
        out_shape=jax.ShapeDtypeStruct((devices, ch, LANES), BF16),
        in_specs=[vmem, vmem, vmem, vmem, smem, smem, vmem],
        out_specs=vmem,
        scratch_shapes=[
            pltpu.VMEM((blocks, LANES, c1), BF16),
            pltpu.VMEM((blocks, ch, LANES), BF16),
            pltpu.VMEM((blocks, ch, LANES), F32),
            pltpu.VMEM((8 * ch, (bins // 8 + 2) * LANES), BF16),
            pltpu.VMEM((80, (bins // 8 + 4) * LANES), BF16),
            pltpu.VMEM((8 * ch, 240), F32),
        ],
        compiler_params=params,
        name="tiles",
    )(all_feats, proj_t, forward, backward, head_weight, entries, targets)
    got = lax.all_to_all(partial, ("row", "col"), 0, 0, tiled=True)
    feat_grad, conv_grad, head_grad, mine = pl.pallas_call(
        functools.partial(finish_kernel, scale, 1.0 / math.sqrt(sequence_length)),
        out_shape=(
            jax.ShapeDtypeStruct(feats.shape, F32),
            jax.ShapeDtypeStruct(conv_t.shape, F32),
            jax.ShapeDtypeStruct((1, ch), F32),
            jax.ShapeDtypeStruct((ch, ch), F32),
        ),
        in_specs=[vmem, vmem, vmem, smem],
        out_specs=(vmem, vmem, vmem, vmem),
        compiler_params=params,
        name="finish",
    )(got, proj_t, conv_t, head_weight)
    other = lax.ppermute(mine, "col", [(c, c ^ 1) for c in range(cols_dev)])
    odd = lax.axis_index("col") % 2 == 1
    proj_grad = jnp.concatenate(
        [jnp.where(odd, other, mine), jnp.where(odd, mine, other)], axis=1
    )
    return feat_grad, proj_grad.T, conv_grad.transpose(1, 0, 2), head_grad.reshape(ch)


def solution(mesh):
    return jax.shard_map(
        body,
        mesh=mesh,
        in_specs=(
            P("row", None, "col", None),
            P(),
            P(),
            P(),
            P("row", "col", None, None),
            P("row", "col", None, None, None),
        ),
        out_specs=(P("row", None, "col", None), P(), P(), P()),
        check_vma=False,
    )
```

```python
import functools
import math

import jax
import jax.numpy as jnp
from jax import lax
from jax.experimental import pallas as pl
from jax.experimental.pallas import tpu as pltpu
from jax.sharding import PartitionSpec as P

DIL = 8
LANES = 128
HALO = 16
F32 = jnp.float32
BF16 = jnp.bfloat16
OUTSIDE = -1e30


def lane_iota(rows):
    return lax.broadcasted_iota(jnp.int32, (rows, LANES), 1)


def split_two(x):
    high = x.astype(BF16).astype(F32)
    return high, x - high


def pad_to(x, rows, cols):
    r, c = x.shape
    if c < cols:
        x = jnp.concatenate([x, jnp.zeros((r, cols - c), x.dtype)], axis=1)
    if r < rows:
        x = jnp.concatenate([x, jnp.zeros((rows - r, cols), x.dtype)], axis=0)
    return x


def column_of(scalars_ref, count):
    sub = lax.broadcasted_iota(jnp.int32, (8, LANES), 0)
    groups = []
    for g in range(count // 8):
        acc = jnp.zeros((8, LANES), F32)
        for k in range(8):
            acc = jnp.where(sub == k, scalars_ref[g * 8 + k], acc)
        groups.append(acc)
    return jnp.concatenate(groups, axis=0)


def taps_kernel(conv_ref, head_ref, table_ref, forward_ref, backward_ref, entries_ref):
    ch = conv_ref.shape[1]
    for s in range(table_ref.shape[3]):
        for k in range(3):
            entries_ref[k, s] = table_ref[0, k, 0, s]
    head_col = column_of(head_ref, ch)
    taps = [
        jnp.sum(head_col[:, :ch] * conv_ref[t].astype(F32), axis=0, keepdims=True)
        for t in range(9)
    ]
    wide = (8, 8 * ch)
    diagonal = lax.broadcasted_iota(jnp.int32, wide, 1) // ch == lax.broadcasted_iota(
        jnp.int32, wide, 0
    )
    hi_tiles, lo_tiles = [
        [
            jnp.where(diagonal, jnp.broadcast_to(jnp.concatenate([row] * 8, axis=1), wide), 0.0)
            for row in rows
        ]
        for rows in zip(*[split_two(row) for row in taps])
    ]
    forward_rows, backward_rows = [], []
    for dy in range(3):
        hi, lo = hi_tiles[3 * dy : 3 * dy + 3], lo_tiles[3 * dy : 3 * dy + 3]
        forward_rows += hi + lo
        backward_rows += hi + hi + lo + [jnp.zeros(wide, F32)]
    forward_taps = jnp.concatenate(forward_rows, axis=0).astype(BF16)
    backward_taps = jnp.transpose(
        jnp.concatenate(backward_rows + [jnp.zeros((16, 8 * ch), F32)], axis=0)
    )[:, :240].astype(BF16)
    forward_ref[...] = forward_taps
    backward_ref[...] = backward_taps


def tiles_kernel(
    rows_dev,
    slots,
    mine_ref,
    other_ref,
    proj_ref,
    forward_ref,
    backward_ref,
    head_ref,
    table_ref,
    targets_ref,
    out_ref,
    fwin_ref,
    gwin_ref,
    dwin_ref,
    u_ref,
    m_ref,
    v_ref,
):
    n_src, chunk, c1 = mine_ref.shape
    odd = lax.axis_index("col") % 2 == 1
    cols_dev = n_src // rows_dev
    blocks = 2 * rows_dev
    bins = cols_dev * chunk
    ch = proj_ref.shape[0]
    lane = lane_iota(ch)
    lane1 = lane_iota(1)

    def chunks_of(b):
        r, half = (b, 0) if b < rows_dev else (blocks - 1 - b, 1)
        first, second = (mine_ref, other_ref) if half == 0 else (other_ref, mine_ref)
        return [
            jnp.where(odd, second[r * cols_dev + c], first[r * cols_dev + c])
            for c in range(cols_dev)
        ]

    zero_halo = jnp.zeros((HALO, c1), BF16)
    for b in range(blocks):
        before = chunks_of(b - 1)[-1][chunk - HALO :] if b > 0 else zero_halo
        after = chunks_of(b + 1)[0][:HALO] if b < blocks - 1 else zero_halo
        tail = jnp.zeros((LANES - bins - 2 * HALO, c1), BF16)
        window = jnp.concatenate([before] + chunks_of(b) + [after, tail], axis=0)
        fwin_ref[b] = window
        g = lax.dot_general(proj_ref[...], window, (((1,), (1,)), ((), ())), preferred_element_type=F32)
        g = 0.5 * g.astype(BF16).astype(F32)
        if b == 0:
            g = jnp.where(lane < HALO, OUTSIDE, g)
        if b == blocks - 1:
            g = jnp.where(lane >= HALO + bins, OUTSIDE, g)
        gwin_ref[b] = g.astype(BF16)
        dwin_ref[b] = jnp.zeros((ch, LANES), F32)

    head_col = column_of(head_ref, ch)
    groups = bins // 8
    m_ref[:, : 2 * LANES] = jnp.zeros((80, 2 * LANES), BF16)
    m_ref[:, (groups + 2) * LANES :] = jnp.zeros((80, 2 * LANES), BF16)
    v_ref[...] = jnp.zeros(v_ref.shape, F32)
    inner = (lane1 >= HALO) & (lane1 < HALO + bins)

    def slot(s, x_acc):
        a, b, live = table_ref[0, s], table_ref[1, s], table_ref[2, s]
        weight = jnp.where(inner, live.astype(F32), 0.0)
        gr, gc = gwin_ref[a].astype(F32), gwin_ref[b].astype(F32)
        pred_r = jnp.sum(jnp.where(lane < HALO + bins, head_col * gr, 0.0), axis=0, keepdims=True)
        pred_c = jnp.sum(jnp.where(lane < HALO + bins, head_col * gc, 0.0), axis=0, keepdims=True)
        pred_r = jnp.transpose(jnp.broadcast_to(pred_r, (LANES, LANES)))

        def activations(g):
            for k in range(8):
                at = HALO - DIL + g * 8 + k
                x = gr[:, at : at + 1] + gc
                u_ref[k * ch : (k + 1) * ch, g * LANES : (g + 1) * LANES] = jnp.maximum(
                    x, 0.0
                ).astype(BF16)
            return jnp.dot(
                forward_ref[...],
                u_ref[:, g * LANES : (g + 1) * LANES],
                preferred_element_type=F32,
            )

        def misfit(c, z):
            terms = []
            for dx in range(3):
                tiles = [
                    z[c + dy][48 * dy + 24 * p + 8 * dx : 48 * dy + 24 * p + 8 * dx + 8]
                    for dy in range(3)
                    for p in range(2)
                ]
                while len(tiles) > 1:
                    tiles = [sum(tiles[i : i + 2]) for i in range(0, len(tiles), 2)]
                terms.append(tiles[0])
            conv = pltpu.roll(terms[0], DIL, 1) + terms[1] + pltpu.roll(terms[2], LANES - DIL, 1)
            goal = targets_ref[0, 0, s, c * 8 : (c + 1) * 8, :]
            goal = jnp.concatenate(
                [jnp.zeros((8, HALO), F32), goal, jnp.zeros((8, LANES - HALO - bins), F32)], axis=1
            )
            at = HALO + c * 8
            m = jnp.where(inner, (conv + pred_c + pred_r[at : at + 8] - goal) * weight, 0.0)
            his, los = [], []
            for moved in (pltpu.roll(m, LANES - DIL, 1), m, pltpu.roll(m, DIL, 1)):
                hi, lo = split_two(moved)
                his.append(hi)
                los.append(lo)
            m_ref[:, (c + 2) * LANES : (c + 3) * LANES] = jnp.concatenate(
                his + los + his + [jnp.zeros((8, LANES), F32)], axis=0
            ).astype(BF16)
            return m

        def gradients(g, d_rows, d_cols):
            cols = slice(g * LANES, (g + 1) * LANES)
            m3 = jnp.concatenate(
                [m_ref[:, (g + 2 - dy) * LANES : (g + 3 - dy) * LANES] for dy in range(3)], axis=0
            )
            up = jnp.dot(backward_ref[...], m3, preferred_element_type=F32)
            grad = jnp.where(u_ref[:, cols].astype(F32) > 0.0, up, 0.0)
            for k in range(8):
                part = grad[k * ch : (k + 1) * ch]
                d_cols = d_cols + part
                d_rows = jnp.where(
                    lane == HALO - DIL + g * 8 + k, jnp.sum(part, axis=1, keepdims=True), d_rows
                )
            return d_rows, d_cols

        z, m_cols, row_sums = [], jnp.zeros((8, LANES), F32), [jnp.zeros((HALO, LANES), F32)]
        d_rows = d_cols = jnp.zeros((ch, LANES), F32)
        for g in range(groups + 2):
            z.append(activations(g))
            if g >= 2:
                m = misfit(g - 2, z)
                m_cols = m_cols + m
                row_sums.append(jnp.broadcast_to(jnp.sum(m, axis=1, keepdims=True), (8, LANES)))
        for g in range(groups + 2):
            d_rows, d_cols = gradients(g, d_rows, d_cols)
        row_sums.append(jnp.zeros((LANES - HALO - bins, LANES), F32))
        m_rows = jnp.transpose(jnp.concatenate(row_sums, axis=0))[:1]
        m_cols = jnp.sum(m_cols, axis=0, keepdims=True)
        frame_cols = (groups + 2) * LANES
        m3 = jnp.concatenate(
            [m_ref[:, (2 - dy) * LANES : (2 - dy) * LANES + frame_cols] for dy in range(3)], axis=0
        )
        v_ref[...] += lax.dot_general(
            u_ref[...], m3, (((1,), (1,)), ((), ())), preferred_element_type=F32
        )
        d_rows = 0.5 * (d_rows + head_col * m_rows)
        d_cols = 0.5 * (d_cols + head_col * m_cols)
        dwin_ref[a] = dwin_ref[a] + d_rows
        dwin_ref[b] = dwin_ref[b] + d_cols
        return x_acc + jnp.where(m_rows != 0.0, gr * m_rows, 0.0) + jnp.where(
            m_cols != 0.0, gc * m_cols, 0.0
        )

    x_acc = lax.fori_loop(0, slots, slot, jnp.zeros((ch, LANES), F32))

    proj_acc = jnp.zeros((2 * ch, c1), F32)
    for b in range(blocks):
        hi, lo = split_two(dwin_ref[b])
        both = jnp.concatenate([hi, lo], axis=0).astype(BF16)
        proj_acc = proj_acc + jnp.dot(both, fwin_ref[b], preferred_element_type=F32)
    proj_acc = pad_to(proj_acc[:ch] + proj_acc[ch:], ch, LANES)

    wide = lax.broadcasted_iota(jnp.int32, (ch, 240), 1)
    v_sum = jnp.zeros((ch, 240), F32)
    for k in range(8):
        v_sum = v_sum + jnp.where(wide % 8 == k, v_ref[k * ch : (k + 1) * ch], 0.0)
    hi, lo = split_two(v_sum)
    source = lax.broadcasted_iota(jnp.int32, (240, LANES), 0)
    place = 2 * ch + 3 * (source // 80) + source % 80 % 24 // 8
    select = (source % 80 < 48) & (lax.broadcasted_iota(jnp.int32, (240, LANES), 1) == place)
    sums = jnp.dot(
        jnp.concatenate([hi, lo], axis=0).astype(BF16),
        select.astype(F32).astype(BF16),
        preferred_element_type=F32,
    )
    sums = sums[:ch] + sums[ch:]
    sums = jnp.where(lane == 2 * ch + 9, jnp.sum(x_acc, axis=1, keepdims=True), sums)
    sums_hi, sums_lo = split_two(sums)
    sums = sums_hi + pltpu.roll(sums_lo, 10, 1)
    shared = [
        jnp.where(lane < 2 * ch, half, sums) for half in (pltpu.roll(proj_acc, ch, 1), proj_acc)
    ]

    def block_gradient(b):
        own = jnp.where((lane >= HALO) & (lane < HALO + bins), dwin_ref[b], 0.0)
        if b > 0:
            before = pltpu.roll(dwin_ref[b - 1], LANES - bins, 1)
            own = own + jnp.where((lane >= HALO) & (lane < HALO + DIL), before, 0.0)
        if b < blocks - 1:
            after = pltpu.roll(dwin_ref[b + 1], bins, 1)
            own = own + jnp.where((lane >= HALO + bins - DIL) & (lane < HALO + bins), after, 0.0)
        return jnp.transpose(pad_to(own, LANES, LANES))[HALO : HALO + bins]

    part = bins // (out_ref.shape[0] // rows_dev)
    lane_part = lane_iota(part)
    for r in range(rows_dev):
        both = (block_gradient(r), block_gradient(blocks - 1 - r))
        for c in range(bins // part):
            dest = r * (bins // part) + c
            base = shared[c % 2]
            for half in range(2):
                rows = slice(half * part, (half + 1) * part)
                piece = jnp.where(
                    lane_part < ch, both[half][c * part : (c + 1) * part], base[rows]
                )
                out_ref[dest, rows] = piece.astype(BF16)
            out_ref[dest, 2 * part :] = base[2 * part :].astype(BF16)


def finish_kernel(
    scale, root, got_ref, proj_ref, conv_ref, head_ref, feat_ref, conv_out_ref, head_out_ref, half_ref
):
    n_src, ch, _ = got_ref.shape
    part = feat_ref.shape[2]
    total = got_ref[0].astype(F32)
    for d in range(1, n_src):
        total = total + got_ref[d].astype(F32)
    half_ref[...] = total[:, ch : 2 * ch] * scale
    whole_t = jnp.transpose(pad_to(total, LANES, LANES))
    proj_t = proj_ref[...]
    hi, lo = split_two(total[: 2 * part, :ch])
    feat = jnp.dot(hi.astype(BF16), proj_t, preferred_element_type=F32) + jnp.dot(
        lo.astype(BF16), proj_t, preferred_element_type=F32
    )
    feat = feat * root
    for half in range(2):
        feat_ref[0, half] = feat[half * part : (half + 1) * part]

    sums = whole_t[2 * ch : 2 * ch + 10, :ch] + whole_t[2 * ch + 10 : 2 * ch + 20, :ch]
    head_col = column_of(head_ref, ch)[:, :ch] * scale
    products = jnp.zeros((ch, ch), F32)
    for t in range(9):
        v = sums[t : t + 1]
        conv_out_ref[t] = head_col * v
        products = products + conv_ref[t].astype(F32) * v
    head_sum = jnp.sum(jnp.transpose(pad_to(products, LANES, LANES)), axis=0, keepdims=True)[:, :ch]
    head_out_ref[...] = (sums[9:10] + head_sum) * scale


def body(feats, proj_weight, conv_weight, head_weight, tile_table, targets):
    rows_dev, cols_dev = lax.axis_size("row"), lax.axis_size("col")
    devices = rows_dev * cols_dev
    _, halves, part, c1 = feats.shape
    ch = proj_weight.shape[1]
    proj_t, conv_t = proj_weight.T, conv_weight.transpose(1, 0, 2)
    bins = part * cols_dev
    blocks = halves * rows_dev
    sequence_length = blocks * bins
    slots = tile_table.shape[2]
    scale = 1.0 / (sequence_length * bins)

    mine = lax.all_to_all(
        jnp.broadcast_to(feats, (devices // halves,) + feats.shape[1:]).reshape(devices, part, c1),
        ("row", "col"),
        0,
        0,
        tiled=True,
    )
    cores = [(c, c ^ 1) for c in range(cols_dev)]
    other = lax.ppermute(mine, "col", cores)
    if part % 16:
        mine, other = mine.reshape(rows_dev, bins, c1), other.reshape(rows_dev, bins, c1)
    vmem = pl.BlockSpec(memory_space=pltpu.VMEM)
    smem = pl.BlockSpec(memory_space=pltpu.SMEM)
    params = pltpu.CompilerParams(vmem_limit_bytes=48 * 1024 * 1024)
    forward, backward, entries = pl.pallas_call(
        taps_kernel,
        out_shape=(
            jax.ShapeDtypeStruct((144, 8 * ch), BF16),
            jax.ShapeDtypeStruct((8 * ch, 240), BF16),
            jax.ShapeDtypeStruct((3, slots), jnp.int32),
        ),
        in_specs=[vmem, smem, smem],
        out_specs=(vmem, vmem, smem),
        compiler_params=params,
        cost_estimate=pl.CostEstimate(flops=10**7, bytes_accessed=10**6, transcendentals=0),
        name="taps",
    )(conv_t, head_weight, tile_table.transpose(0, 3, 1, 2))
    partial = pl.pallas_call(
        functools.partial(tiles_kernel, rows_dev, slots),
        out_shape=jax.ShapeDtypeStruct((devices, ch, LANES), BF16),
        in_specs=[vmem, vmem, vmem, vmem, vmem, smem, smem, vmem],
        out_specs=vmem,
        scratch_shapes=[
            pltpu.VMEM((blocks, LANES, c1), BF16),
            pltpu.VMEM((blocks, ch, LANES), BF16),
            pltpu.VMEM((blocks, ch, LANES), F32),
            pltpu.VMEM((8 * ch, (bins // 8 + 2) * LANES), BF16),
            pltpu.VMEM((80, (bins // 8 + 4) * LANES), BF16),
            pltpu.VMEM((8 * ch, 240), F32),
        ],
        compiler_params=params,
        name="tiles",
    )(mine, other, proj_t, forward, backward, head_weight, entries, targets)
    got = lax.all_to_all(partial, ("row", "col"), 0, 0, tiled=True)
    feat_grad, conv_grad, head_grad, own_part = pl.pallas_call(
        functools.partial(finish_kernel, scale, 1.0 / math.sqrt(sequence_length)),
        out_shape=(
            jax.ShapeDtypeStruct(feats.shape, F32),
            jax.ShapeDtypeStruct(conv_t.shape, F32),
            jax.ShapeDtypeStruct((1, ch), F32),
            jax.ShapeDtypeStruct((ch, ch), F32),
        ),
        in_specs=[vmem, vmem, vmem, smem],
        out_specs=(vmem, vmem, vmem, vmem),
        compiler_params=params,
        name="finish",
    )(got, proj_t, conv_t, head_weight)
    other_part = lax.ppermute(own_part, "col", cores)
    odd = lax.axis_index("col") % 2 == 1
    proj_grad = jnp.concatenate(
        [jnp.where(odd, other_part, own_part), jnp.where(odd, own_part, other_part)], axis=1
    )
    return feat_grad, proj_grad.T, conv_grad.transpose(1, 0, 2), head_grad.reshape(ch)


def solution(mesh):
    return jax.shard_map(
        body,
        mesh=mesh,
        in_specs=(
            P("row", None, "col", None),
            P(),
            P(),
            P(),
            P("row", "col", None, None),
            P("row", "col", None, None, None),
        ),
        out_specs=(P("row", None, "col", None), P(), P(), P()),
        check_vma=False,
    )
```

```python
import functools
import math

import jax
import jax.numpy as jnp
from jax import lax
from jax.experimental import pallas as pl
from jax.experimental.pallas import tpu as pltpu
from jax.sharding import PartitionSpec as P

DIL = 8
LANES = 128
HALO = 16
F32 = jnp.float32
BF16 = jnp.bfloat16
OUTSIDE = -1e30


def lane_iota(rows):
    return lax.broadcasted_iota(jnp.int32, (rows, LANES), 1)


def split_two(x):
    high = x.astype(BF16).astype(F32)
    return high, x - high


def pad_to(x, rows, cols):
    r, c = x.shape
    if c < cols:
        x = jnp.concatenate([x, jnp.zeros((r, cols - c), x.dtype)], axis=1)
    if r < rows:
        x = jnp.concatenate([x, jnp.zeros((rows - r, cols), x.dtype)], axis=0)
    return x


def column_of(scalars_ref, count):
    sub = lax.broadcasted_iota(jnp.int32, (8, LANES), 0)
    groups = []
    for g in range(count // 8):
        acc = jnp.zeros((8, LANES), F32)
        for k in range(8):
            acc = jnp.where(sub == k, scalars_ref[g * 8 + k], acc)
        groups.append(acc)
    return jnp.concatenate(groups, axis=0)


def taps_kernel(conv_ref, head_ref, table_ref, forward_ref, backward_ref, entries_ref):
    ch = conv_ref.shape[1]
    for s in range(table_ref.shape[3]):
        for k in range(3):
            entries_ref[k, s] = table_ref[0, k, 0, s]
    head_col = column_of(head_ref, ch)
    taps = [
        jnp.sum(head_col[:, :ch] * conv_ref[t].astype(F32), axis=0, keepdims=True)
        for t in range(9)
    ]
    wide = (8, 8 * ch)
    diagonal = lax.broadcasted_iota(jnp.int32, wide, 1) // ch == lax.broadcasted_iota(
        jnp.int32, wide, 0
    )
    hi_tiles, lo_tiles = [
        [
            jnp.where(diagonal, jnp.broadcast_to(jnp.concatenate([row] * 8, axis=1), wide), 0.0)
            for row in rows
        ]
        for rows in zip(*[split_two(row) for row in taps])
    ]
    forward_rows, backward_rows = [], []
    for dy in range(3):
        hi, lo = hi_tiles[3 * dy : 3 * dy + 3], lo_tiles[3 * dy : 3 * dy + 3]
        forward_rows += hi + lo
        backward_rows += hi + hi + lo + [jnp.zeros(wide, F32)]
    forward_taps = jnp.concatenate(forward_rows, axis=0).astype(BF16)
    backward_taps = jnp.transpose(
        jnp.concatenate(backward_rows + [jnp.zeros((16, 8 * ch), F32)], axis=0)
    )[:, :240].astype(BF16)
    forward_ref[...] = forward_taps
    backward_ref[...] = backward_taps


def tiles_kernel(
    rows_dev,
    slots,
    mine_ref,
    other_ref,
    proj_ref,
    forward_ref,
    backward_ref,
    head_ref,
    table_ref,
    targets_ref,
    out_ref,
    fwin_ref,
    gwin_ref,
    dwin_ref,
    u_ref,
    m_ref,
    v_ref,
):
    n_src, chunk, c1 = mine_ref.shape
    odd = lax.axis_index("col") % 2 == 1
    cols_dev = n_src // rows_dev
    blocks = 2 * rows_dev
    bins = cols_dev * chunk
    ch = proj_ref.shape[0]
    lane = lane_iota(ch)
    lane1 = lane_iota(1)

    def chunks_of(b):
        r, half = (b, 0) if b < rows_dev else (blocks - 1 - b, 1)
        first, second = (mine_ref, other_ref) if half == 0 else (other_ref, mine_ref)
        return [
            jnp.where(odd, second[r * cols_dev + c], first[r * cols_dev + c])
            for c in range(cols_dev)
        ]

    zero_halo = jnp.zeros((HALO, c1), BF16)
    for b in range(blocks):
        before = chunks_of(b - 1)[-1][chunk - HALO :] if b > 0 else zero_halo
        after = chunks_of(b + 1)[0][:HALO] if b < blocks - 1 else zero_halo
        tail = jnp.zeros((LANES - bins - 2 * HALO, c1), BF16)
        window = jnp.concatenate([before] + chunks_of(b) + [after, tail], axis=0)
        fwin_ref[b] = window
        g = lax.dot_general(proj_ref[...], window, (((1,), (1,)), ((), ())), preferred_element_type=F32)
        g = 0.5 * g.astype(BF16).astype(F32)
        if b == 0:
            g = jnp.where(lane < HALO, OUTSIDE, g)
        if b == blocks - 1:
            g = jnp.where(lane >= HALO + bins, OUTSIDE, g)
        gwin_ref[b] = g.astype(BF16)
        dwin_ref[b] = jnp.zeros((ch, LANES), F32)

    head_col = column_of(head_ref, ch)
    groups = bins // 8
    m_ref[:, : 2 * LANES] = jnp.zeros((80, 2 * LANES), BF16)
    m_ref[:, (groups + 2) * LANES :] = jnp.zeros((80, 2 * LANES), BF16)
    v_ref[...] = jnp.zeros(v_ref.shape, F32)
    inner = (lane1 >= HALO) & (lane1 < HALO + bins)

    def slot(s, x_acc):
        a, b, live = table_ref[0, s], table_ref[1, s], table_ref[2, s]
        weight = jnp.where(inner, live.astype(F32), 0.0)
        gr, gc = gwin_ref[a].astype(F32), gwin_ref[b].astype(F32)
        pred_r = jnp.sum(jnp.where(lane < HALO + bins, head_col * gr, 0.0), axis=0, keepdims=True)
        pred_c = jnp.sum(jnp.where(lane < HALO + bins, head_col * gc, 0.0), axis=0, keepdims=True)
        pred_r = jnp.transpose(jnp.broadcast_to(pred_r, (LANES, LANES)))

        def activations(g):
            for k in range(8):
                at = HALO - DIL + g * 8 + k
                x = gr[:, at : at + 1] + gc
                u_ref[k * ch : (k + 1) * ch, g * LANES : (g + 1) * LANES] = jnp.maximum(
                    x, 0.0
                ).astype(BF16)
            return jnp.dot(
                forward_ref[...],
                u_ref[:, g * LANES : (g + 1) * LANES],
                preferred_element_type=F32,
            )

        def misfit(c, z):
            terms = []
            for dx in range(3):
                tiles = [
                    z[c + dy][48 * dy + 24 * p + 8 * dx : 48 * dy + 24 * p + 8 * dx + 8]
                    for dy in range(3)
                    for p in range(2)
                ]
                while len(tiles) > 1:
                    tiles = [sum(tiles[i : i + 2]) for i in range(0, len(tiles), 2)]
                terms.append(tiles[0])
            conv = pltpu.roll(terms[0], DIL, 1) + terms[1] + pltpu.roll(terms[2], LANES - DIL, 1)
            goal = targets_ref[0, 0, s, c * 8 : (c + 1) * 8, :]
            goal = jnp.concatenate(
                [jnp.zeros((8, HALO), F32), goal, jnp.zeros((8, LANES - HALO - bins), F32)], axis=1
            )
            at = HALO + c * 8
            m = jnp.where(inner, (conv + pred_c + pred_r[at : at + 8] - goal) * weight, 0.0)
            his, los = [], []
            for moved in (pltpu.roll(m, LANES - DIL, 1), m, pltpu.roll(m, DIL, 1)):
                hi, lo = split_two(moved)
                his.append(hi)
                los.append(lo)
            m_ref[:, (c + 2) * LANES : (c + 3) * LANES] = jnp.concatenate(
                his + los + his + [jnp.zeros((8, LANES), F32)], axis=0
            ).astype(BF16)
            return m

        def gradients(g, d_rows, d_cols):
            cols = slice(g * LANES, (g + 1) * LANES)
            m3 = jnp.concatenate(
                [m_ref[:, (g + 2 - dy) * LANES : (g + 3 - dy) * LANES] for dy in range(3)], axis=0
            )
            up = jnp.dot(backward_ref[...], m3, preferred_element_type=F32)
            grad = jnp.where(u_ref[:, cols].astype(F32) > 0.0, up, 0.0)
            for k in range(8):
                part = grad[k * ch : (k + 1) * ch]
                d_cols = d_cols + part
                d_rows = jnp.where(
                    lane == HALO - DIL + g * 8 + k, jnp.sum(part, axis=1, keepdims=True), d_rows
                )
            return d_rows, d_cols

        z, m_cols, row_sums = [], jnp.zeros((8, LANES), F32), [jnp.zeros((HALO, LANES), F32)]
        d_rows = d_cols = jnp.zeros((ch, LANES), F32)
        for g in range(groups + 2):
            z.append(activations(g))
            if g >= 2:
                m = misfit(g - 2, z)
                m_cols = m_cols + m
                row_sums.append(jnp.broadcast_to(jnp.sum(m, axis=1, keepdims=True), (8, LANES)))
        for g in range(groups + 2):
            d_rows, d_cols = gradients(g, d_rows, d_cols)
        row_sums.append(jnp.zeros((LANES - HALO - bins, LANES), F32))
        m_rows = jnp.transpose(jnp.concatenate(row_sums, axis=0))[:1]
        m_cols = jnp.sum(m_cols, axis=0, keepdims=True)
        frame_cols = (groups + 2) * LANES
        m3 = jnp.concatenate(
            [m_ref[:, (2 - dy) * LANES : (2 - dy) * LANES + frame_cols] for dy in range(3)], axis=0
        )
        v_ref[...] += lax.dot_general(
            u_ref[...], m3, (((1,), (1,)), ((), ())), preferred_element_type=F32
        )
        d_rows = 0.5 * (d_rows + head_col * m_rows)
        d_cols = 0.5 * (d_cols + head_col * m_cols)
        dwin_ref[a] = dwin_ref[a] + d_rows
        dwin_ref[b] = dwin_ref[b] + d_cols
        return x_acc + jnp.where(m_rows != 0.0, gr * m_rows, 0.0) + jnp.where(
            m_cols != 0.0, gc * m_cols, 0.0
        )

    x_acc = lax.fori_loop(0, slots, slot, jnp.zeros((ch, LANES), F32))

    proj_acc = jnp.zeros((2 * ch, c1), F32)
    for b in range(blocks):
        hi, lo = split_two(dwin_ref[b])
        both = jnp.concatenate([hi, lo], axis=0).astype(BF16)
        proj_acc = proj_acc + jnp.dot(both, fwin_ref[b], preferred_element_type=F32)
    proj_acc = pad_to(proj_acc[:ch] + proj_acc[ch:], ch, LANES)

    wide = lax.broadcasted_iota(jnp.int32, (ch, 240), 1)
    v_sum = jnp.zeros((ch, 240), F32)
    for k in range(8):
        v_sum = v_sum + jnp.where(wide % 8 == k, v_ref[k * ch : (k + 1) * ch], 0.0)
    hi, lo = split_two(v_sum)
    source = lax.broadcasted_iota(jnp.int32, (240, LANES), 0)
    place = 2 * ch + 3 * (source // 80) + source % 80 % 24 // 8
    select = (source % 80 < 48) & (lax.broadcasted_iota(jnp.int32, (240, LANES), 1) == place)
    sums = jnp.dot(
        jnp.concatenate([hi, lo], axis=0).astype(BF16),
        select.astype(F32).astype(BF16),
        preferred_element_type=F32,
    )
    sums = sums[:ch] + sums[ch:]
    sums = jnp.where(lane == 2 * ch + 9, jnp.sum(x_acc, axis=1, keepdims=True), sums)
    shared = []
    lane32, low16 = lane_iota(32), slice(32, 48)
    for k in range(2):
        half = pltpu.roll(proj_acc, ch - ch * k, 1) if k == 0 else proj_acc
        tail = jnp.concatenate(
            [pltpu.roll(half[low16], 48, 1), pltpu.roll(half[low16], 24, 1)], axis=0
        )
        v_head = pltpu.roll(sums[:32], 24 - 5 * k, 1)
        v_tail = jnp.concatenate(
            [pltpu.roll(sums[low16], 29 - 5 * k, 1), pltpu.roll(sums[low16], 26 - 5 * k, 1)], axis=0
        )
        shared.append(
            jnp.where(
                lane32 < 96,
                half[:32],
                jnp.where(lane32 < 120, tail, jnp.where(lane32 < 125, v_head, v_tail)),
            )
        )

    def block_gradient(b):
        own = jnp.where((lane >= HALO) & (lane < HALO + bins), dwin_ref[b], 0.0)
        if b > 0:
            before = pltpu.roll(dwin_ref[b - 1], LANES - bins, 1)
            own = own + jnp.where((lane >= HALO) & (lane < HALO + DIL), before, 0.0)
        if b < blocks - 1:
            after = pltpu.roll(dwin_ref[b + 1], bins, 1)
            own = own + jnp.where((lane >= HALO + bins - DIL) & (lane < HALO + bins), after, 0.0)
        return jnp.transpose(pad_to(own, LANES, LANES))[HALO : HALO + bins]

    part = bins // (out_ref.shape[0] // rows_dev)
    lane_part = lane_iota(part)
    for r in range(rows_dev):
        both = (block_gradient(r), block_gradient(blocks - 1 - r))
        for c in range(bins // part):
            dest = r * (bins // part) + c
            base = shared[c % 2]
            for half in range(2):
                rows = slice(half * part, (half + 1) * part)
                piece = jnp.where(
                    lane_part < ch, both[half][c * part : (c + 1) * part], base[rows]
                )
                out_ref[dest, rows] = piece.astype(BF16)
            if 2 * part < 32:
                out_ref[dest, 2 * part :] = base[2 * part :].astype(BF16)


def total_kernel(root, got_ref, proj_ref, feat_ref, total_ref):
    n_src = got_ref.shape[0]
    ch = proj_ref.shape[0]
    part = feat_ref.shape[2]
    totals = [got_ref[d].astype(F32) for d in range(4)]
    for d in range(4, n_src):
        totals[d % 4] = totals[d % 4] + got_ref[d].astype(F32)
    total = (totals[0] + totals[1]) + (totals[2] + totals[3])
    total_ref[...] = total
    hi, lo = split_two(total[: 2 * part, :ch])
    feat = jnp.dot(
        jnp.concatenate([hi, lo], axis=0).astype(BF16), proj_ref[...], preferred_element_type=F32
    )
    for half in range(2):
        rows = slice(half * part, (half + 1) * part)
        feat_ref[0, half] = (feat[: 2 * part][rows] + feat[2 * part :][rows]) * root


def weights_kernel(scale, mine_ref, other_ref, conv_ref, head_ref, proj_out_ref, conv_out_ref, head_out_ref):
    ch = conv_ref.shape[1]
    odd = lax.axis_index("col") % 2 == 1
    mine, other = mine_ref[...], other_ref[...]
    lane16, lane32 = lane_iota(16), lane_iota(32)

    heads, tails, v_heads, v_tails = [], [], [], []
    for k, part in enumerate((jnp.where(odd, other, mine), jnp.where(odd, mine, other))):
        heads.append(pltpu.roll(part, 80, 1) if k == 0 else part)
        tails.append([pltpu.roll(part[:16], 32 + 48 * k, 1), pltpu.roll(part[16:], 56 + 48 * k, 1)])
        v_heads.append(pltpu.roll(part, 8 + 5 * k, 1))
        v_tails.append([pltpu.roll(part[:16], 3 + 5 * k, 1), pltpu.roll(part[16:], 6 + 5 * k, 1)])
    head = jnp.where(lane32 < 48, heads[0], heads[1])
    tail = jnp.where(
        lane16 < 48,
        jnp.where(lane16 < 24, tails[0][0], tails[0][1]),
        jnp.where(lane16 < 72, tails[1][0], tails[1][1]),
    )
    proj_out_ref[...] = jnp.concatenate([head, tail], axis=0)[:, : 2 * ch] * scale
    v_head = jnp.where(lane32 < 5, v_heads[0], v_heads[1])
    v_tail = jnp.where(
        lane16 < 5,
        jnp.where(lane16 < 3, v_tails[0][0], v_tails[0][1]),
        jnp.where(lane16 < 8, v_tails[1][0], v_tails[1][1]),
    )
    sums = jnp.concatenate([v_head, v_tail], axis=0)
    sums = jnp.transpose(pad_to(sums, LANES, LANES))[:10, :ch]
    head_col = column_of(head_ref, ch)[:, :ch] * scale
    products = jnp.zeros((ch, ch), F32)
    for t in range(9):
        v = sums[t : t + 1]
        conv_out_ref[t] = head_col * v
        products = products + conv_ref[t].astype(F32) * v
    head_sum = jnp.sum(jnp.transpose(pad_to(products, LANES, LANES)), axis=0, keepdims=True)[:, :ch]
    head_out_ref[...] = (sums[9:10] + head_sum) * scale


def body(feats, proj_weight, conv_weight, head_weight, tile_table, targets):
    rows_dev, cols_dev = lax.axis_size("row"), lax.axis_size("col")
    devices = rows_dev * cols_dev
    _, halves, part, c1 = feats.shape
    ch = proj_weight.shape[1]
    proj_t, conv_t = proj_weight.T, conv_weight.transpose(1, 0, 2)
    bins = part * cols_dev
    blocks = halves * rows_dev
    sequence_length = blocks * bins
    slots = tile_table.shape[2]
    scale = 1.0 / (sequence_length * bins)

    mine = lax.all_to_all(
        jnp.broadcast_to(feats, (devices // halves,) + feats.shape[1:]).reshape(devices, part, c1),
        ("row", "col"),
        0,
        0,
        tiled=True,
    )
    cores = [(c, c ^ 1) for c in range(cols_dev)]
    other = lax.ppermute(mine, "col", cores)
    if part % 16:
        mine, other = mine.reshape(rows_dev, bins, c1), other.reshape(rows_dev, bins, c1)
    vmem = pl.BlockSpec(memory_space=pltpu.VMEM)
    smem = pl.BlockSpec(memory_space=pltpu.SMEM)
    params = pltpu.CompilerParams(vmem_limit_bytes=48 * 1024 * 1024)
    forward, backward, entries = pl.pallas_call(
        taps_kernel,
        out_shape=(
            jax.ShapeDtypeStruct((144, 8 * ch), BF16),
            jax.ShapeDtypeStruct((8 * ch, 240), BF16),
            jax.ShapeDtypeStruct((3, slots), jnp.int32),
        ),
        in_specs=[vmem, smem, smem],
        out_specs=(vmem, vmem, smem),
        compiler_params=params,
        cost_estimate=pl.CostEstimate(flops=10**7, bytes_accessed=10**6, transcendentals=0),
        name="taps",
    )(conv_t, head_weight, tile_table.transpose(0, 3, 1, 2))
    partial = pl.pallas_call(
        functools.partial(tiles_kernel, rows_dev, slots),
        out_shape=jax.ShapeDtypeStruct((devices, 32, LANES), BF16),
        in_specs=[vmem, vmem, vmem, vmem, vmem, smem, smem, vmem],
        out_specs=vmem,
        scratch_shapes=[
            pltpu.VMEM((blocks, LANES, c1), BF16),
            pltpu.VMEM((blocks, ch, LANES), BF16),
            pltpu.VMEM((blocks, ch, LANES), F32),
            pltpu.VMEM((8 * ch, (bins // 8 + 2) * LANES), BF16),
            pltpu.VMEM((80, (bins // 8 + 4) * LANES), BF16),
            pltpu.VMEM((8 * ch, 240), F32),
        ],
        compiler_params=params,
        name="tiles",
    )(mine, other, proj_t, forward, backward, head_weight, entries, targets)
    got = lax.all_to_all(partial, ("row", "col"), 0, 0, tiled=True)
    feat_grad, own_total = pl.pallas_call(
        functools.partial(total_kernel, 1.0 / math.sqrt(sequence_length)),
        out_shape=(
            jax.ShapeDtypeStruct(feats.shape, F32),
            jax.ShapeDtypeStruct((32, LANES), F32),
        ),
        in_specs=[vmem, vmem],
        out_specs=(vmem, vmem),
        compiler_params=params,
        name="total",
    )(got, proj_t)
    other_total = lax.ppermute(own_total, "col", cores)
    proj_grad, conv_grad, head_grad = pl.pallas_call(
        functools.partial(weights_kernel, scale),
        out_shape=(
            jax.ShapeDtypeStruct(proj_t.shape, F32),
            jax.ShapeDtypeStruct(conv_t.shape, F32),
            jax.ShapeDtypeStruct((1, ch), F32),
        ),
        in_specs=[vmem, vmem, vmem, smem],
        out_specs=(vmem, vmem, vmem),
        compiler_params=params,
        name="weights",
    )(own_total, other_total, conv_t, head_weight)
    return feat_grad, proj_grad.T, conv_grad.transpose(1, 0, 2), head_grad.reshape(ch)


def solution(mesh):
    return jax.shard_map(
        body,
        mesh=mesh,
        in_specs=(
            P("row", None, "col", None),
            P(),
            P(),
            P(),
            P("row", "col", None, None),
            P("row", "col", None, None, None),
        ),
        out_specs=(P("row", None, "col", None), P(), P(), P()),
        check_vma=False,
    )
```

```python
import functools
import math

import jax
import jax.numpy as jnp
from jax import lax
from jax.experimental import pallas as pl
from jax.experimental.pallas import tpu as pltpu
from jax.sharding import PartitionSpec as P

DIL = 8
LANES = 128
HALO = 16
F32 = jnp.float32
BF16 = jnp.bfloat16
OUTSIDE = -1e30


def lane_iota(rows):
    return lax.broadcasted_iota(jnp.int32, (rows, LANES), 1)


def split_two(x):
    high = x.astype(BF16).astype(F32)
    return high, x - high


def pad_to(x, rows, cols):
    r, c = x.shape
    if c < cols:
        x = jnp.concatenate([x, jnp.zeros((r, cols - c), x.dtype)], axis=1)
    if r < rows:
        x = jnp.concatenate([x, jnp.zeros((rows - r, cols), x.dtype)], axis=0)
    return x


def column_of(scalars_ref, count):
    sub = lax.broadcasted_iota(jnp.int32, (8, LANES), 0)
    groups = []
    for g in range(count // 8):
        acc = jnp.zeros((8, LANES), F32)
        for k in range(8):
            acc = jnp.where(sub == k, scalars_ref[g * 8 + k], acc)
        groups.append(acc)
    return jnp.concatenate(groups, axis=0)


def taps_kernel(conv_ref, head_ref, table_ref, forward_ref, backward_ref, column_ref, entries_ref):
    ch = conv_ref.shape[1]
    for s in range(table_ref.shape[3]):
        for k in range(3):
            entries_ref[k, s] = table_ref[0, k, 0, s]
    head_col = column_of(head_ref, ch)
    taps = [
        jnp.sum(head_col[:, :ch] * conv_ref[t].astype(F32), axis=0, keepdims=True)
        for t in range(9)
    ]
    wide = (8, 8 * ch)
    diagonal = lax.broadcasted_iota(jnp.int32, wide, 1) // ch == lax.broadcasted_iota(
        jnp.int32, wide, 0
    )
    hi_tiles, lo_tiles = [
        [
            jnp.where(diagonal, jnp.broadcast_to(jnp.concatenate([row] * 8, axis=1), wide), 0.0)
            for row in rows
        ]
        for rows in zip(*[split_two(row) for row in taps])
    ]
    forward_rows, backward_rows = [], []
    for dy in range(3):
        hi, lo = hi_tiles[3 * dy : 3 * dy + 3], lo_tiles[3 * dy : 3 * dy + 3]
        forward_rows += hi + lo
        backward_rows += hi + lo
    forward_taps = jnp.concatenate(forward_rows, axis=0).astype(BF16)
    pad = [jnp.zeros((112, 8 * ch), F32)]
    backward_taps = jnp.transpose(jnp.concatenate(backward_rows + pad, axis=0))[:, :144].astype(BF16)
    forward_ref[...] = forward_taps
    backward_ref[...] = backward_taps
    column_ref[...] = head_col


def tiles_kernel(
    rows_dev,
    slots,
    mine_ref,
    other_ref,
    proj_ref,
    forward_ref,
    backward_ref,
    column_ref,
    table_ref,
    targets_ref,
    keep_ref,
    give_ref,
    fwin_ref,
    gwin_ref,
    dwin_ref,
    u_ref,
    m_ref,
    v_ref,
):
    n_src, chunk, c1 = mine_ref.shape
    odd = lax.axis_index("col") % 2 == 1
    cols_dev = n_src // rows_dev
    blocks = 2 * rows_dev
    bins = cols_dev * chunk
    ch = proj_ref.shape[0]
    lane = lane_iota(ch)
    lane1 = lane_iota(1)

    def chunks_of(b):
        r, half = (b, 0) if b < rows_dev else (blocks - 1 - b, 1)
        first, second = (mine_ref, other_ref) if half == 0 else (other_ref, mine_ref)
        return [
            jnp.where(odd, second[r * cols_dev + c], first[r * cols_dev + c])
            for c in range(cols_dev)
        ]

    zero_halo = jnp.zeros((HALO, c1), BF16)
    for b in range(blocks):
        before = chunks_of(b - 1)[-1][chunk - HALO :] if b > 0 else zero_halo
        after = chunks_of(b + 1)[0][:HALO] if b < blocks - 1 else zero_halo
        tail = jnp.zeros((LANES - bins - 2 * HALO, c1), BF16)
        window = jnp.concatenate([before] + chunks_of(b) + [after, tail], axis=0)
        fwin_ref[b] = window
        g = lax.dot_general(proj_ref[...], window, (((1,), (1,)), ((), ())), preferred_element_type=F32)
        g = 0.5 * g.astype(BF16).astype(F32)
        if b == 0:
            g = jnp.where(lane < HALO, OUTSIDE, g)
        if b == blocks - 1:
            g = jnp.where(lane >= HALO + bins, OUTSIDE, g)
        gwin_ref[b] = g.astype(BF16)
        dwin_ref[b] = jnp.zeros((ch, LANES), F32)

    head_col = column_ref[...]
    groups = bins // 8
    m_ref[:, : 2 * LANES] = jnp.zeros((48, 2 * LANES), BF16)
    m_ref[:, (groups + 2) * LANES :] = jnp.zeros((48, 2 * LANES), BF16)
    v_ref[...] = jnp.zeros(v_ref.shape, F32)
    inner = (lane1 >= HALO) & (lane1 < HALO + bins)

    def slot(s, x_acc):
        a, b, live = table_ref[0, s], table_ref[1, s], table_ref[2, s]
        weight = jnp.where(inner, live.astype(F32), 0.0)
        gr, gc = gwin_ref[a].astype(F32), gwin_ref[b].astype(F32)
        pred_r = jnp.sum(jnp.where(lane < HALO + bins, head_col * gr, 0.0), axis=0, keepdims=True)
        pred_c = jnp.sum(jnp.where(lane < HALO + bins, head_col * gc, 0.0), axis=0, keepdims=True)
        pred_r = jnp.transpose(jnp.broadcast_to(pred_r, (LANES, LANES)))

        def activations(g):
            for k in range(8):
                at = HALO - DIL + g * 8 + k
                x = gr[:, at : at + 1] + gc
                u_ref[k * ch : (k + 1) * ch, g * LANES : (g + 1) * LANES] = jnp.maximum(
                    x, 0.0
                ).astype(BF16)
            return jnp.dot(
                forward_ref[...],
                u_ref[:, g * LANES : (g + 1) * LANES],
                preferred_element_type=F32,
            )

        def misfit(c, z):
            terms = []
            for dx in range(3):
                tiles = [
                    z[c + dy][48 * dy + 24 * p + 8 * dx : 48 * dy + 24 * p + 8 * dx + 8]
                    for dy in range(3)
                    for p in range(2)
                ]
                while len(tiles) > 1:
                    tiles = [sum(tiles[i : i + 2]) for i in range(0, len(tiles), 2)]
                terms.append(tiles[0])
            conv = pltpu.roll(terms[0], DIL, 1) + terms[1] + pltpu.roll(terms[2], LANES - DIL, 1)
            goal = targets_ref[0, 0, s, c * 8 : (c + 1) * 8, :]
            goal = jnp.concatenate(
                [jnp.zeros((8, HALO), F32), goal, jnp.zeros((8, LANES - HALO - bins), F32)], axis=1
            )
            at = HALO + c * 8
            m = jnp.where(inner, (conv + pred_c + pred_r[at : at + 8] - goal) * weight, 0.0)
            moved = [pltpu.roll(m, LANES - DIL, 1), m, pltpu.roll(m, DIL, 1)]
            m_ref[:, (c + 2) * LANES : (c + 3) * LANES] = jnp.concatenate(
                moved + moved, axis=0
            ).astype(BF16)
            return m

        def gradients(g, d_rows, d_cols):
            cols = slice(g * LANES, (g + 2) * LANES)
            m3 = jnp.concatenate(
                [m_ref[:, (g + 2 - dy) * LANES : (g + 4 - dy) * LANES] for dy in range(3)], axis=0
            )
            up = jnp.dot(backward_ref[...], m3, preferred_element_type=F32)
            grad = jnp.where(u_ref[:, cols].astype(F32) > 0.0, up, 0.0)
            for k in range(16):
                at = slice(k // 8 * LANES, (k // 8 + 1) * LANES)
                part = grad[k % 8 * ch : (k % 8 + 1) * ch, at]
                d_cols = d_cols + part
                d_rows = jnp.where(
                    lane == HALO - DIL + g * 8 + k, jnp.sum(part, axis=1, keepdims=True), d_rows
                )
            return d_rows, d_cols

        z, m_cols, row_sums = [], jnp.zeros((8, LANES), F32), [jnp.zeros((HALO, LANES), F32)]
        d_rows = d_cols = jnp.zeros((ch, LANES), F32)
        for g in range(groups + 2):
            z.append(activations(g))
            if g >= 2:
                m = misfit(g - 2, z)
                m_cols = m_cols + m
                row_sums.append(jnp.broadcast_to(jnp.sum(m, axis=1, keepdims=True), (8, LANES)))
        for g in range(0, groups + 2, 2):
            d_rows, d_cols = gradients(g, d_rows, d_cols)
        row_sums.append(jnp.zeros((LANES - HALO - bins, LANES), F32))
        m_rows = jnp.transpose(jnp.concatenate(row_sums, axis=0))[:1]
        m_cols = jnp.sum(m_cols, axis=0, keepdims=True)
        frame_cols = (groups + 2) * LANES
        m3 = jnp.concatenate(
            [m_ref[:32, (2 - dy) * LANES : (2 - dy) * LANES + frame_cols] for dy in range(3)], axis=0
        )
        v_ref[...] += lax.dot_general(
            m3, u_ref[...], (((1,), (1,)), ((), ())), preferred_element_type=F32
        )
        d_rows = 0.5 * (d_rows + head_col * m_rows)
        d_cols = 0.5 * (d_cols + head_col * m_cols)
        dwin_ref[a] = dwin_ref[a] + d_rows
        dwin_ref[b] = dwin_ref[b] + d_cols
        return x_acc + jnp.where(m_rows != 0.0, gr * m_rows, 0.0) + jnp.where(
            m_cols != 0.0, gc * m_cols, 0.0
        )

    x_acc = lax.fori_loop(0, slots, slot, jnp.zeros((ch, LANES), F32))

    proj_acc = jnp.zeros((2 * ch, c1), F32)
    for b in range(blocks):
        hi, lo = split_two(dwin_ref[b])
        both = jnp.concatenate([hi, lo], axis=0).astype(BF16)
        proj_acc = proj_acc + jnp.dot(both, fwin_ref[b], preferred_element_type=F32)
    proj_acc = pad_to(proj_acc[:ch] + proj_acc[ch:], ch, LANES)

    wide = (96, 8 * ch)
    own_row = lax.broadcasted_iota(jnp.int32, wide, 0) % 8 == (
        lax.broadcasted_iota(jnp.int32, wide, 1) // ch
    )
    hi, lo = split_two(jnp.where(own_row, v_ref[...], 0.0))
    source = lax.broadcasted_iota(jnp.int32, (16, 96), 1)
    place = 3 * (source // 32) + source % 32 // 8
    select = (source % 32 < 24) & (lax.broadcasted_iota(jnp.int32, (16, 96), 0) == place)
    select = select.astype(F32).astype(BF16)
    v_rows = jnp.dot(select, hi.astype(BF16), preferred_element_type=F32) + jnp.dot(
        select, lo.astype(BF16), preferred_element_type=F32
    )
    v_sum = v_rows[:, :ch]
    for k in range(1, 8):
        v_sum = v_sum + v_rows[:, k * ch : (k + 1) * ch]
    sums = pltpu.roll(jnp.transpose(pad_to(v_sum, LANES, LANES))[:ch], 2 * ch, 1)
    sums = jnp.where(lane == 2 * ch + 9, jnp.sum(x_acc, axis=1, keepdims=True), sums)
    def block_gradient(b):
        own = dwin_ref[b]
        at_start, at_end = lane < HALO + DIL, lane >= HALO + bins - DIL
        if b > 0:
            own = own + jnp.where(at_start, pltpu.roll(dwin_ref[b - 1], LANES - bins, 1), 0.0)
        if b < blocks - 1:
            own = own + jnp.where(at_end, pltpu.roll(dwin_ref[b + 1], bins, 1), 0.0)
        return own

    for j in range(rows_dev // 2):
        packs = []
        for half in range(2):
            b0, b1 = [r if half == 0 else blocks - 1 - r for r in (2 * j, 2 * j + 1)]
            first = pltpu.roll(block_gradient(b0), LANES - HALO, 1)
            second = pltpu.roll(block_gradient(b1), bins - HALO, 1)
            packs.append(jnp.where(lane < bins, first, second))
        keep_ref[j] = jnp.where(odd, packs[1], packs[0])
        give_ref[j] = jnp.where(odd, packs[0], packs[1])
    weights = jnp.where(lane < 2 * ch, proj_acc, sums)
    keep_ref[rows_dev // 2] = weights
    give_ref[rows_dev // 2] = weights


def pair_kernel(keep_ref, took_ref, out_ref):
    pairs, ch = keep_ref.shape[0] - 1, keep_ref.shape[1]
    odd = lax.axis_index("col") % 2 == 1
    bins = LANES // 2
    cols_dev = out_ref.shape[0] // (2 * pairs)
    part = bins // cols_dev
    weights = keep_ref[pairs] + took_ref[pairs]
    chunks = [weights[16 * q : 16 * q + 16] for q in range(3)]
    lane16 = lane_iota(16)

    def share(dest, k):
        first = 48 * dest + 24 * k
        moved = [pltpu.roll(chunks[q], (48 + 24 * q - first) % LANES, 1) for q in range(3)]
        v_own = pltpu.roll(chunks[2 * k], 24 - 5 * dest, 1)
        v_middle = pltpu.roll(chunks[1], 29 - 5 * dest - 3 * k, 1)
        out = jnp.where(lane16 < 125, v_own, v_middle)
        for q in (2, 1, 0):
            out = jnp.where(lane16 < 72 + 24 * q, moved[q], out)
        return out

    shares = [jnp.where(odd, share(dest, 1), share(dest, 0)) for dest in range(2)]
    lane_part = lane_iota(part)
    for j in range(pairs):
        both = jnp.transpose(pad_to(keep_ref[j] + took_ref[j], LANES, LANES))
        for i in range(2 * cols_dev):
            dest = 2 * j * cols_dev + i
            base = shares[i % 2]
            rows = both[i * part : (i + 1) * part]
            out_ref[dest, :part] = jnp.where(lane_part < ch, rows, base[:part]).astype(BF16)
            if part < 16:
                out_ref[dest, part:] = base[part:].astype(BF16)


def total_kernel(got_ref, total_ref):
    totals = [got_ref[d].astype(F32) for d in range(4)]
    for d in range(4, got_ref.shape[0]):
        totals[d % 4] = totals[d % 4] + got_ref[d].astype(F32)
    total_ref[:16] = totals[0] + totals[2]
    total_ref[16:] = totals[1] + totals[3]


def features_kernel(root, total_ref, proj_ref, feat_ref):
    ch = proj_ref.shape[0]
    part = feat_ref.shape[2]
    rows = [total_ref[16 * half : 16 * half + part, :ch] for half in range(2)]
    hi, lo = split_two(jnp.concatenate(rows, axis=0))
    feat = jnp.dot(
        jnp.concatenate([hi, lo], axis=0).astype(BF16), proj_ref[...], preferred_element_type=F32
    )
    for half in range(2):
        at = half * part
        feat_ref[0, half] = (feat[at : at + part] + feat[2 * part + at : 3 * part + at]) * root


def weights_kernel(scale, mine_ref, other_ref, conv_ref, column_ref, proj_out_ref, conv_out_ref, head_out_ref):
    ch = conv_ref.shape[1]
    odd = lax.axis_index("col") % 2 == 1
    mine, other = mine_ref[...], other_ref[...]
    lane16 = lane_iota(16)
    parts = (jnp.where(odd, other, mine), jnp.where(odd, mine, other))

    def sent(dest, k, shift):
        return pltpu.roll(parts[dest][16 * k : 16 * k + 16], shift % LANES, 1)

    proj_rows = []
    for q in range(3):
        rows = sent(1, 1, 72 - 48 - 24 * q)
        for n in (2, 1, 0):
            rows = jnp.where(lane16 < 24 * n + 24, sent(n // 2, n % 2, 24 * n - 48 - 24 * q), rows)
        proj_rows.append(rows)
    proj_out_ref[...] = jnp.concatenate(proj_rows, axis=0)[:, : 2 * ch] * scale
    v_rows = []
    for q in range(3):
        by_dest = []
        for dest in range(2):
            if q == 1:
                first, second = sent(dest, 0, 5 * dest - 125), sent(dest, 1, 5 * dest + 3 - 125)
                by_dest.append(jnp.where(lane16 < 5 * dest + 3, first, second))
            else:
                by_dest.append(sent(dest, q // 2, 5 * dest - 120))
        v_rows.append(jnp.where(lane16 < 5, by_dest[0], by_dest[1]))
    sums = jnp.concatenate(v_rows, axis=0)
    sums = jnp.transpose(pad_to(sums, LANES, LANES))[:10, :ch]
    head_col = column_ref[:, :ch] * scale
    products = jnp.zeros((ch, ch), F32)
    for t in range(9):
        v = sums[t : t + 1]
        conv_out_ref[t] = head_col * v
        products = products + conv_ref[t].astype(F32) * v
    head_sum = jnp.sum(jnp.transpose(pad_to(products, LANES, LANES)), axis=0, keepdims=True)[:, :ch]
    head_out_ref[...] = (sums[9:10] + head_sum) * scale


def body(feats, proj_weight, conv_weight, head_weight, tile_table, targets):
    rows_dev, cols_dev = lax.axis_size("row"), lax.axis_size("col")
    devices = rows_dev * cols_dev
    _, halves, part, c1 = feats.shape
    ch = proj_weight.shape[1]
    proj_t, conv_t = proj_weight.T, conv_weight.transpose(1, 0, 2)
    bins = part * cols_dev
    blocks = halves * rows_dev
    sequence_length = blocks * bins
    slots = tile_table.shape[2]
    scale = 1.0 / (sequence_length * bins)

    mine = lax.all_to_all(
        jnp.broadcast_to(feats, (devices // halves,) + feats.shape[1:]).reshape(devices, part, c1),
        ("row", "col"),
        0,
        0,
        tiled=True,
    )
    cores = [(c, c ^ 1) for c in range(cols_dev)]
    other = lax.ppermute(mine, "col", cores)
    if part % 16:
        mine, other = mine.reshape(rows_dev, bins, c1), other.reshape(rows_dev, bins, c1)
    vmem = pl.BlockSpec(memory_space=pltpu.VMEM)
    smem = pl.BlockSpec(memory_space=pltpu.SMEM)
    params = pltpu.CompilerParams(vmem_limit_bytes=48 * 1024 * 1024)
    forward, backward, head_column, entries = pl.pallas_call(
        taps_kernel,
        out_shape=(
            jax.ShapeDtypeStruct((144, 8 * ch), BF16),
            jax.ShapeDtypeStruct((8 * ch, 144), BF16),
            jax.ShapeDtypeStruct((ch, LANES), F32),
            jax.ShapeDtypeStruct((3, slots), jnp.int32),
        ),
        in_specs=[vmem, smem, smem],
        out_specs=(vmem, vmem, vmem, smem),
        compiler_params=params,
        cost_estimate=pl.CostEstimate(flops=10**7, bytes_accessed=10**6, transcendentals=0),
        name="taps",
    )(conv_t, head_weight, tile_table.transpose(0, 3, 1, 2))
    keep, give = pl.pallas_call(
        functools.partial(tiles_kernel, rows_dev, slots),
        out_shape=(jax.ShapeDtypeStruct((rows_dev // 2 + 1, ch, LANES), F32),) * 2,
        in_specs=[vmem, vmem, vmem, vmem, vmem, vmem, smem, vmem],
        out_specs=(vmem, vmem),
        scratch_shapes=[
            pltpu.VMEM((blocks, LANES, c1), BF16),
            pltpu.VMEM((blocks, ch, LANES), BF16),
            pltpu.VMEM((blocks, ch, LANES), F32),
            pltpu.VMEM((8 * ch, (bins // 8 + 2) * LANES), BF16),
            pltpu.VMEM((48, (bins // 8 + 4) * LANES), BF16),
            pltpu.VMEM((96, 8 * ch), F32),
        ],
        compiler_params=params,
        name="tiles",
    )(mine, other, proj_t, forward, backward, head_column, entries, targets)
    took = lax.ppermute(give, "col", cores)
    partial = pl.pallas_call(
        pair_kernel,
        out_shape=jax.ShapeDtypeStruct((devices, 16, LANES), BF16),
        in_specs=[vmem, vmem],
        out_specs=vmem,
        compiler_params=params,
        name="pair",
    )(keep, took)
    got = lax.all_to_all(partial, ("row", "col"), 0, 0, tiled=True)
    own_total = pl.pallas_call(
        total_kernel,
        out_shape=jax.ShapeDtypeStruct((32, LANES), F32),
        in_specs=[vmem],
        out_specs=vmem,
        compiler_params=params,
        name="total",
    )(got)
    other_total = lax.ppermute(own_total, "col", cores)
    feat_grad = pl.pallas_call(
        functools.partial(features_kernel, 1.0 / math.sqrt(sequence_length)),
        out_shape=jax.ShapeDtypeStruct(feats.shape, F32),
        in_specs=[vmem, vmem],
        out_specs=vmem,
        compiler_params=params,
        cost_estimate=pl.CostEstimate(flops=10**7, bytes_accessed=10**6, transcendentals=0),
        name="features",
    )(own_total, proj_t)
    proj_grad, conv_grad, head_grad = pl.pallas_call(
        functools.partial(weights_kernel, scale),
        out_shape=(
            jax.ShapeDtypeStruct(proj_t.shape, F32),
            jax.ShapeDtypeStruct(conv_t.shape, F32),
            jax.ShapeDtypeStruct((1, ch), F32),
        ),
        in_specs=[vmem, vmem, vmem, vmem],
        out_specs=(vmem, vmem, vmem),
        compiler_params=params,
        name="weights",
    )(own_total, other_total, conv_t, head_column)
    return feat_grad, proj_grad.T, conv_grad.transpose(1, 0, 2), head_grad.reshape(ch)


def solution(mesh):
    return jax.shard_map(
        body,
        mesh=mesh,
        in_specs=(
            P("row", None, "col", None),
            P(),
            P(),
            P(),
            P("row", "col", None, None),
            P("row", "col", None, None, None),
        ),
        out_specs=(P("row", None, "col", None), P(), P(), P()),
        check_vma=False,
    )
```

```python
import functools
import math

import jax
import jax.numpy as jnp
from jax import lax
from jax.experimental import pallas as pl
from jax.experimental.pallas import tpu as pltpu
from jax.sharding import PartitionSpec as P

DIL = 8
LANES = 128
HALO = 16
F32 = jnp.float32
BF16 = jnp.bfloat16
OUTSIDE = -1e30


def lane_iota(rows):
    return lax.broadcasted_iota(jnp.int32, (rows, LANES), 1)


def split_two(x):
    high = x.astype(BF16).astype(F32)
    return high, x - high


def pad_to(x, rows, cols):
    r, c = x.shape
    if c < cols:
        x = jnp.concatenate([x, jnp.zeros((r, cols - c), x.dtype)], axis=1)
    if r < rows:
        x = jnp.concatenate([x, jnp.zeros((rows - r, cols), x.dtype)], axis=0)
    return x


def taps_kernel(conv_ref, head_ref, table_ref, forward_ref, backward_ref, column_ref, entries_ref):
    ch = conv_ref.shape[1]
    entries_ref[...] = pad_to(table_ref[0, :, 0, :], 8, LANES)
    head_col = jnp.transpose(jnp.broadcast_to(pad_to(head_ref[...], 1, LANES), (LANES, LANES)))[:ch]
    taps = [
        jnp.sum(head_col[:, :ch] * conv_ref[t].astype(F32), axis=0, keepdims=True)
        for t in range(9)
    ]
    wide = (8, 8 * ch)
    diagonal = lax.broadcasted_iota(jnp.int32, wide, 1) // ch == lax.broadcasted_iota(
        jnp.int32, wide, 0
    )
    hi_tiles, lo_tiles = [
        [
            jnp.where(diagonal, jnp.broadcast_to(jnp.concatenate([row] * 8, axis=1), wide), 0.0)
            for row in rows
        ]
        for rows in zip(*[split_two(row) for row in taps])
    ]
    forward_rows, backward_rows = [], []
    for dy in range(3):
        hi, lo = hi_tiles[3 * dy : 3 * dy + 3], lo_tiles[3 * dy : 3 * dy + 3]
        forward_rows += hi + lo
        backward_rows += hi + lo
    forward_taps = jnp.concatenate(forward_rows, axis=0).astype(BF16)
    pad = [jnp.zeros((112, 8 * ch), F32)]
    backward_taps = jnp.transpose(jnp.concatenate(backward_rows + pad, axis=0))[:, :144].astype(BF16)
    forward_ref[...] = forward_taps
    backward_ref[...] = backward_taps
    column_ref[...] = head_col


def tiles_kernel(
    rows_dev,
    slots,
    mine_ref,
    other_ref,
    proj_ref,
    forward_ref,
    backward_ref,
    column_ref,
    entries_ref,
    targets_ref,
    keep_ref,
    give_ref,
    fwin_ref,
    gwin_ref,
    dwin_ref,
    u_ref,
    m_ref,
    v_ref,
    table_ref,
    table_sem,
):
    table_copy = pltpu.make_async_copy(entries_ref, table_ref, table_sem)
    table_copy.start()
    n_src, chunk, c1 = mine_ref.shape
    odd = lax.axis_index("col") % 2 == 1
    cols_dev = n_src // rows_dev
    blocks = 2 * rows_dev
    bins = cols_dev * chunk
    ch = proj_ref.shape[0]
    lane = lane_iota(ch)
    lane1 = lane_iota(1)

    def chunks_of(b):
        r, half = (b, 0) if b < rows_dev else (blocks - 1 - b, 1)
        first, second = (mine_ref, other_ref) if half == 0 else (other_ref, mine_ref)
        return [
            jnp.where(odd, second[r * cols_dev + c], first[r * cols_dev + c])
            for c in range(cols_dev)
        ]

    zero_halo = jnp.zeros((HALO, c1), BF16)
    for b in range(blocks):
        before = chunks_of(b - 1)[-1][chunk - HALO :] if b > 0 else zero_halo
        after = chunks_of(b + 1)[0][:HALO] if b < blocks - 1 else zero_halo
        tail = jnp.zeros((LANES - bins - 2 * HALO, c1), BF16)
        window = jnp.concatenate([before] + chunks_of(b) + [after, tail], axis=0)
        fwin_ref[b] = window
        g = lax.dot_general(proj_ref[...], window, (((1,), (1,)), ((), ())), preferred_element_type=F32)
        g = 0.5 * g.astype(BF16).astype(F32)
        if b == 0:
            g = jnp.where(lane < HALO, OUTSIDE, g)
        if b == blocks - 1:
            g = jnp.where(lane >= HALO + bins, OUTSIDE, g)
        gwin_ref[b] = g.astype(BF16)
        dwin_ref[b] = jnp.zeros((ch, LANES), F32)

    head_col = column_ref[...]
    groups = bins // 8
    m_ref[:, : 2 * LANES] = jnp.zeros((48, 2 * LANES), BF16)
    m_ref[:, (groups + 2) * LANES :] = jnp.zeros((48, 2 * LANES), BF16)
    v_ref[...] = jnp.zeros(v_ref.shape, F32)
    inner = (lane1 >= HALO) & (lane1 < HALO + bins)

    def slot(s, x_acc):
        a, b, live = table_ref[0, s], table_ref[1, s], table_ref[2, s]
        weight = jnp.where(inner, live.astype(F32), 0.0)
        gr, gc = gwin_ref[a].astype(F32), gwin_ref[b].astype(F32)
        pred_r = jnp.sum(jnp.where(lane < HALO + bins, head_col * gr, 0.0), axis=0, keepdims=True)
        pred_c = jnp.sum(jnp.where(lane < HALO + bins, head_col * gc, 0.0), axis=0, keepdims=True)
        pred_r = jnp.transpose(jnp.broadcast_to(pred_r, (LANES, LANES)))

        def activations(g):
            for k in range(8):
                at = HALO - DIL + g * 8 + k
                x = gr[:, at : at + 1] + gc
                u_ref[k * ch : (k + 1) * ch, g * LANES : (g + 1) * LANES] = jnp.maximum(
                    x, 0.0
                ).astype(BF16)

        def misfit(c, z):
            terms = []
            for dx in range(3):
                tiles = [
                    z[c + dy][48 * dy + 24 * p + 8 * dx : 48 * dy + 24 * p + 8 * dx + 8]
                    for dy in range(3)
                    for p in range(2)
                ]
                while len(tiles) > 1:
                    tiles = [sum(tiles[i : i + 2]) for i in range(0, len(tiles), 2)]
                terms.append(tiles[0])
            conv = pltpu.roll(terms[0], DIL, 1) + terms[1] + pltpu.roll(terms[2], LANES - DIL, 1)
            goal = targets_ref[0, 0, s, c * 8 : (c + 1) * 8, :]
            goal = jnp.concatenate(
                [jnp.zeros((8, HALO), F32), goal, jnp.zeros((8, LANES - HALO - bins), F32)], axis=1
            )
            at = HALO + c * 8
            m = jnp.where(inner, (conv + pred_c + pred_r[at : at + 8] - goal) * weight, 0.0)
            moved = [pltpu.roll(m, LANES - DIL, 1), m, pltpu.roll(m, DIL, 1)]
            m_ref[:, (c + 2) * LANES : (c + 3) * LANES] = jnp.concatenate(
                moved + moved, axis=0
            ).astype(BF16)
            return m

        def gradients(g, d_rows, d_cols):
            cols = slice(g * LANES, (g + 2) * LANES)
            m3 = jnp.concatenate(
                [m_ref[:, (g + 2 - dy) * LANES : (g + 4 - dy) * LANES] for dy in range(3)], axis=0
            )
            up = jnp.dot(backward_ref[...], m3, preferred_element_type=F32)
            grad = jnp.where(u_ref[:, cols].astype(F32) > 0.0, up, 0.0)
            for k in range(16):
                at = slice(k // 8 * LANES, (k // 8 + 1) * LANES)
                part = grad[k % 8 * ch : (k % 8 + 1) * ch, at]
                d_cols = d_cols + part
                d_rows = jnp.where(
                    lane == HALO - DIL + g * 8 + k, jnp.sum(part, axis=1, keepdims=True), d_rows
                )
            return d_rows, d_cols

        z, m_cols, row_sums = [], jnp.zeros((8, LANES), F32), [jnp.zeros((HALO, LANES), F32)]
        d_rows = d_cols = jnp.zeros((ch, LANES), F32)
        def next_misfit(c, m_cols):
            m = misfit(c, z)
            row_sums.append(jnp.broadcast_to(jnp.sum(m, axis=1, keepdims=True), (8, LANES)))
            return m_cols + m

        def tap_sums(g):
            m3 = jnp.concatenate(
                [m_ref[:32, (g + 2 - dy) * LANES : (g + 4 - dy) * LANES] for dy in range(3)], axis=0
            )
            v_ref[...] += lax.dot_general(
                m3,
                u_ref[:, g * LANES : (g + 2) * LANES],
                (((1,), (1,)), ((), ())),
                preferred_element_type=F32,
            )

        for g in range(0, groups + 2, 2):
            activations(g)
            activations(g + 1)
            pair = jnp.dot(
                forward_ref[...],
                u_ref[:, g * LANES : (g + 2) * LANES],
                preferred_element_type=F32,
            )
            z += [pair[:, :LANES], pair[:, LANES:]]
        for c in range(groups // 2):
            m_cols = next_misfit(c, m_cols)
        for g in range(0, groups + 2, 2):
            d_rows, d_cols = gradients(g, d_rows, d_cols)
            tap_sums(g)
            for c in (groups // 2 + g, groups // 2 + g + 1):
                if c < groups:
                    m_cols = next_misfit(c, m_cols)
        row_sums.append(jnp.zeros((LANES - HALO - bins, LANES), F32))
        m_rows = jnp.transpose(jnp.concatenate(row_sums, axis=0))[:1]
        m_cols = jnp.sum(m_cols, axis=0, keepdims=True)
        d_rows = 0.5 * (d_rows + head_col * m_rows)
        d_cols = 0.5 * (d_cols + head_col * m_cols)
        dwin_ref[a] = dwin_ref[a] + d_rows
        dwin_ref[b] = dwin_ref[b] + d_cols
        return x_acc + jnp.where(m_rows != 0.0, gr * m_rows, 0.0) + jnp.where(
            m_cols != 0.0, gc * m_cols, 0.0
        )

    table_copy.wait()
    x_acc = lax.fori_loop(0, slots, slot, jnp.zeros((ch, LANES), F32))

    proj_acc = jnp.zeros((2 * ch, c1), F32)
    for b in range(blocks):
        hi, lo = split_two(dwin_ref[b])
        both = jnp.concatenate([hi, lo], axis=0).astype(BF16)
        proj_acc = proj_acc + jnp.dot(both, fwin_ref[b], preferred_element_type=F32)
    proj_acc = pad_to(proj_acc[:ch] + proj_acc[ch:], ch, LANES)

    wide = (96, 8 * ch)
    own_row = lax.broadcasted_iota(jnp.int32, wide, 0) % 8 == (
        lax.broadcasted_iota(jnp.int32, wide, 1) // ch
    )
    hi, lo = split_two(jnp.where(own_row, v_ref[...], 0.0))
    source = lax.broadcasted_iota(jnp.int32, (16, 96), 1)
    place = 3 * (source // 32) + source % 32 // 8
    select = (source % 32 < 24) & (lax.broadcasted_iota(jnp.int32, (16, 96), 0) == place)
    select = select.astype(F32).astype(BF16)
    v_rows = jnp.dot(select, hi.astype(BF16), preferred_element_type=F32) + jnp.dot(
        select, lo.astype(BF16), preferred_element_type=F32
    )
    v_sum = v_rows[:, :ch]
    for k in range(1, 8):
        v_sum = v_sum + v_rows[:, k * ch : (k + 1) * ch]
    sums = pltpu.roll(jnp.transpose(pad_to(v_sum, LANES, LANES))[:ch], 2 * ch, 1)
    sums = jnp.where(lane == 2 * ch + 9, jnp.sum(x_acc, axis=1, keepdims=True), sums)
    def block_gradient(b):
        own = dwin_ref[b]
        at_start, at_end = lane < HALO + DIL, lane >= HALO + bins - DIL
        if b > 0:
            own = own + jnp.where(at_start, pltpu.roll(dwin_ref[b - 1], LANES - bins, 1), 0.0)
        if b < blocks - 1:
            own = own + jnp.where(at_end, pltpu.roll(dwin_ref[b + 1], bins, 1), 0.0)
        return own

    for j in range(rows_dev // 2):
        packs = []
        for half in range(2):
            b0, b1 = [r if half == 0 else blocks - 1 - r for r in (2 * j, 2 * j + 1)]
            first = pltpu.roll(block_gradient(b0), LANES - HALO, 1)
            second = pltpu.roll(block_gradient(b1), bins - HALO, 1)
            packs.append(jnp.where(lane < bins, first, second))
        keep_ref[j] = jnp.where(odd, packs[1], packs[0])
        give_ref[j] = jnp.where(odd, packs[0], packs[1])
    weights = jnp.where(lane < 2 * ch, proj_acc, sums)
    keep_ref[rows_dev // 2] = weights
    give_ref[rows_dev // 2] = weights


def pair_kernel(keep_ref, took_ref, out_ref):
    pairs, ch = keep_ref.shape[0] - 1, keep_ref.shape[1]
    odd = lax.axis_index("col") % 2 == 1
    bins = LANES // 2
    cols_dev = out_ref.shape[0] // (2 * pairs)
    part = bins // cols_dev
    weights = keep_ref[pairs] + took_ref[pairs]
    chunks = [weights[16 * q : 16 * q + 16] for q in range(3)]
    lane16 = lane_iota(16)

    def share(dest, k):
        first = 48 * dest + 24 * k
        moved = [pltpu.roll(chunks[q], (48 + 24 * q - first) % LANES, 1) for q in range(3)]
        v_own = pltpu.roll(chunks[2 * k], 24 - 5 * dest, 1)
        v_middle = pltpu.roll(chunks[1], 29 - 5 * dest - 3 * k, 1)
        out = jnp.where(lane16 < 125, v_own, v_middle)
        for q in (2, 1, 0):
            out = jnp.where(lane16 < 72 + 24 * q, moved[q], out)
        return out

    shares = [jnp.where(odd, share(dest, 1), share(dest, 0)) for dest in range(2)]
    lane_part = lane_iota(part)
    for j in range(pairs):
        both = jnp.transpose(pad_to(keep_ref[j] + took_ref[j], LANES, LANES))
        for i in range(2 * cols_dev):
            dest = 2 * j * cols_dev + i
            base = shares[i % 2]
            rows = both[i * part : (i + 1) * part]
            out_ref[dest, :part] = jnp.where(lane_part < ch, rows, base[:part]).astype(BF16)
            if part < 16:
                out_ref[dest, part:] = base[part:].astype(BF16)


def total_kernel(got_ref, total_ref):
    totals = [got_ref[d].astype(F32) for d in range(4)]
    for d in range(4, got_ref.shape[0]):
        totals[d % 4] = totals[d % 4] + got_ref[d].astype(F32)
    total_ref[:16] = totals[0] + totals[2]
    total_ref[16:] = totals[1] + totals[3]


def features_kernel(root, total_ref, proj_ref, feat_ref):
    ch = proj_ref.shape[0]
    part = feat_ref.shape[2]
    rows = [total_ref[16 * half : 16 * half + part, :ch] for half in range(2)]
    hi, lo = split_two(jnp.concatenate(rows, axis=0))
    feat = jnp.dot(
        jnp.concatenate([hi, lo], axis=0).astype(BF16), proj_ref[...], preferred_element_type=F32
    )
    for half in range(2):
        at = half * part
        feat_ref[0, half] = (feat[at : at + part] + feat[2 * part + at : 3 * part + at]) * root


def weights_kernel(scale, mine_ref, other_ref, conv_ref, column_ref, proj_out_ref, conv_out_ref, head_out_ref):
    ch = conv_ref.shape[1]
    odd = lax.axis_index("col") % 2 == 1
    mine, other = mine_ref[...], other_ref[...]
    lane16 = lane_iota(16)
    parts = (jnp.where(odd, other, mine), jnp.where(odd, mine, other))

    def sent(dest, k, shift):
        return pltpu.roll(parts[dest][16 * k : 16 * k + 16], shift % LANES, 1)

    proj_rows = []
    for q in range(3):
        rows = sent(1, 1, 72 - 48 - 24 * q)
        for n in (2, 1, 0):
            rows = jnp.where(lane16 < 24 * n + 24, sent(n // 2, n % 2, 24 * n - 48 - 24 * q), rows)
        proj_rows.append(rows)
    proj_out_ref[...] = jnp.concatenate(proj_rows, axis=0)[:, : 2 * ch] * scale
    v_rows = []
    for q in range(3):
        by_dest = []
        for dest in range(2):
            if q == 1:
                first, second = sent(dest, 0, 5 * dest - 125), sent(dest, 1, 5 * dest + 3 - 125)
                by_dest.append(jnp.where(lane16 < 5 * dest + 3, first, second))
            else:
                by_dest.append(sent(dest, q // 2, 5 * dest - 120))
        v_rows.append(jnp.where(lane16 < 5, by_dest[0], by_dest[1]))
    sums = jnp.concatenate(v_rows, axis=0)
    sums = jnp.transpose(pad_to(sums, LANES, LANES))[:10, :ch]
    head_col = column_ref[:, :ch] * scale
    products = jnp.zeros((ch, ch), F32)
    for t in range(9):
        v = sums[t : t + 1]
        conv_out_ref[t] = head_col * v
        products = products + conv_ref[t].astype(F32) * v
    head_sum = jnp.sum(jnp.transpose(pad_to(products, LANES, LANES)), axis=0, keepdims=True)[:, :ch]
    head_out_ref[...] = (sums[9:10] + head_sum) * scale


def body(feats, proj_weight, conv_weight, head_weight, tile_table, targets):
    rows_dev, cols_dev = lax.axis_size("row"), lax.axis_size("col")
    devices = rows_dev * cols_dev
    _, halves, part, c1 = feats.shape
    ch = proj_weight.shape[1]
    proj_t, conv_t = proj_weight.T, conv_weight.transpose(1, 0, 2)
    bins = part * cols_dev
    blocks = halves * rows_dev
    sequence_length = blocks * bins
    slots = tile_table.shape[2]
    scale = 1.0 / (sequence_length * bins)

    mine = lax.all_to_all(
        jnp.broadcast_to(feats, (devices // halves,) + feats.shape[1:]).reshape(devices, part, c1),
        ("row", "col"),
        0,
        0,
        tiled=True,
    )
    cores = [(c, c ^ 1) for c in range(cols_dev)]
    other = lax.ppermute(mine, "col", cores)
    if part % 16:
        mine, other = mine.reshape(rows_dev, bins, c1), other.reshape(rows_dev, bins, c1)
    vmem = pl.BlockSpec(memory_space=pltpu.VMEM)
    params = pltpu.CompilerParams(vmem_limit_bytes=48 * 1024 * 1024)
    forward, backward, head_column, entries = pl.pallas_call(
        taps_kernel,
        out_shape=(
            jax.ShapeDtypeStruct((144, 8 * ch), BF16),
            jax.ShapeDtypeStruct((8 * ch, 144), BF16),
            jax.ShapeDtypeStruct((ch, LANES), F32),
            jax.ShapeDtypeStruct((8, LANES), jnp.int32),
        ),
        in_specs=[vmem, vmem, vmem],
        out_specs=(vmem, vmem, vmem, vmem),
        compiler_params=params,
        cost_estimate=pl.CostEstimate(flops=10**7, bytes_accessed=10**6, transcendentals=0),
        name="taps",
    )(conv_t, head_weight.reshape(1, ch), tile_table.transpose(0, 3, 1, 2))
    keep, give = pl.pallas_call(
        functools.partial(tiles_kernel, rows_dev, slots),
        out_shape=(jax.ShapeDtypeStruct((rows_dev // 2 + 1, ch, LANES), F32),) * 2,
        in_specs=[vmem] * 8,
        out_specs=(vmem, vmem),
        scratch_shapes=[
            pltpu.VMEM((blocks, LANES, c1), BF16),
            pltpu.VMEM((blocks, ch, LANES), BF16),
            pltpu.VMEM((blocks, ch, LANES), F32),
            pltpu.VMEM((8 * ch, (bins // 8 + 2) * LANES), BF16),
            pltpu.VMEM((48, (bins // 8 + 4) * LANES), BF16),
            pltpu.VMEM((96, 8 * ch), F32),
            pltpu.SMEM((8, LANES), jnp.int32),
            pltpu.SemaphoreType.DMA,
        ],
        compiler_params=params,
        name="tiles",
    )(mine, other, proj_t, forward, backward, head_column, entries, targets)
    took = lax.ppermute(give, "col", cores)
    partial = pl.pallas_call(
        pair_kernel,
        out_shape=jax.ShapeDtypeStruct((devices, 16, LANES), BF16),
        in_specs=[vmem, vmem],
        out_specs=vmem,
        compiler_params=params,
        name="pair",
    )(keep, took)
    got = lax.all_to_all(partial, ("row", "col"), 0, 0, tiled=True)
    own_total = pl.pallas_call(
        total_kernel,
        out_shape=jax.ShapeDtypeStruct((32, LANES), F32),
        in_specs=[vmem],
        out_specs=vmem,
        compiler_params=params,
        name="total",
    )(got)
    other_total = lax.ppermute(own_total, "col", cores)
    feat_grad = pl.pallas_call(
        functools.partial(features_kernel, 1.0 / math.sqrt(sequence_length)),
        out_shape=jax.ShapeDtypeStruct(feats.shape, F32),
        in_specs=[vmem, vmem],
        out_specs=vmem,
        compiler_params=params,
        cost_estimate=pl.CostEstimate(flops=10**7, bytes_accessed=10**6, transcendentals=0),
        name="features",
    )(own_total, proj_t)
    proj_grad, conv_grad, head_grad = pl.pallas_call(
        functools.partial(weights_kernel, scale),
        out_shape=(
            jax.ShapeDtypeStruct(proj_t.shape, F32),
            jax.ShapeDtypeStruct(conv_t.shape, F32),
            jax.ShapeDtypeStruct((1, ch), F32),
        ),
        in_specs=[vmem, vmem, vmem, vmem],
        out_specs=(vmem, vmem, vmem),
        compiler_params=params,
        name="weights",
    )(own_total, other_total, conv_t, head_column)
    return feat_grad, proj_grad.T, conv_grad.transpose(1, 0, 2), head_grad.reshape(ch)


def solution(mesh):
    return jax.shard_map(
        body,
        mesh=mesh,
        in_specs=(
            P("row", None, "col", None),
            P(),
            P(),
            P(),
            P("row", "col", None, None),
            P("row", "col", None, None, None),
        ),
        out_specs=(P("row", None, "col", None), P(), P(), P()),
        check_vma=False,
    )
```

```python
import functools
import math

import jax
import jax.numpy as jnp
from jax import lax
from jax.experimental import pallas as pl
from jax.experimental.pallas import tpu as pltpu
from jax.sharding import PartitionSpec as P

DIL = 8
LANES = 128
HALO = 16
F32 = jnp.float32
BF16 = jnp.bfloat16
OUTSIDE = -1e30


def lane_iota(rows):
    return lax.broadcasted_iota(jnp.int32, (rows, LANES), 1)


def split_two(x):
    high = x.astype(BF16).astype(F32)
    return high, x - high


def pad_to(x, rows, cols):
    r, c = x.shape
    if c < cols:
        x = jnp.concatenate([x, jnp.zeros((r, cols - c), x.dtype)], axis=1)
    if r < rows:
        x = jnp.concatenate([x, jnp.zeros((rows - r, cols), x.dtype)], axis=0)
    return x


def taps_kernel(conv_ref, head_ref, table_ref, forward_ref, backward_ref, column_ref, entries_ref):
    ch = conv_ref.shape[1]
    entries_ref[...] = pad_to(table_ref[0, :, 0, :], 8, LANES)
    head_col = jnp.transpose(jnp.broadcast_to(pad_to(head_ref[...], 1, LANES), (LANES, LANES)))[:ch]
    taps = [
        jnp.sum(head_col[:, :ch] * conv_ref[t].astype(F32), axis=0, keepdims=True)
        for t in range(9)
    ]
    wide = (8, 8 * ch)
    diagonal = lax.broadcasted_iota(jnp.int32, wide, 1) // ch == lax.broadcasted_iota(
        jnp.int32, wide, 0
    )
    hi_tiles, lo_tiles = [
        [
            jnp.where(diagonal, jnp.broadcast_to(jnp.concatenate([row] * 8, axis=1), wide), 0.0)
            for row in rows
        ]
        for rows in zip(*[split_two(row) for row in taps])
    ]
    forward_rows, backward_rows = [], []
    for dy in range(3):
        hi, lo = hi_tiles[3 * dy : 3 * dy + 3], lo_tiles[3 * dy : 3 * dy + 3]
        forward_rows += hi + lo
        backward_rows += hi + lo
    forward_taps = jnp.concatenate(forward_rows, axis=0).astype(BF16)
    pad = [jnp.zeros((112, 8 * ch), F32)]
    backward_taps = jnp.transpose(jnp.concatenate(backward_rows + pad, axis=0))[:, :144].astype(BF16)
    forward_ref[...] = forward_taps
    backward_ref[...] = backward_taps
    column_ref[...] = head_col


def tiles_kernel(
    rows_dev,
    slots,
    mine_ref,
    other_ref,
    proj_ref,
    forward_ref,
    backward_ref,
    column_ref,
    entries_ref,
    targets_ref,
    keep_ref,
    give_ref,
    fwin_ref,
    gwin_ref,
    dwin_ref,
    u_ref,
    m_ref,
    v_ref,
    table_ref,
    table_sem,
):
    table_copy = pltpu.make_async_copy(entries_ref, table_ref, table_sem)
    table_copy.start()
    n_src, chunk, c1 = mine_ref.shape
    odd = lax.axis_index("col") % 2 == 1
    cols_dev = n_src // rows_dev
    blocks = 2 * rows_dev
    bins = cols_dev * chunk
    ch = proj_ref.shape[0]
    lane = lane_iota(ch)
    lane1 = lane_iota(1)

    def chunks_of(b):
        r, half = (b, 0) if b < rows_dev else (blocks - 1 - b, 1)
        first, second = (mine_ref, other_ref) if half == 0 else (other_ref, mine_ref)
        return [
            jnp.where(odd, second[r * cols_dev + c], first[r * cols_dev + c])
            for c in range(cols_dev)
        ]

    zero_halo = jnp.zeros((HALO, c1), BF16)
    for b in range(blocks):
        before = chunks_of(b - 1)[-1][chunk - HALO :] if b > 0 else zero_halo
        after = chunks_of(b + 1)[0][:HALO] if b < blocks - 1 else zero_halo
        tail = jnp.zeros((LANES - bins - 2 * HALO, c1), BF16)
        window = jnp.concatenate([before] + chunks_of(b) + [after, tail], axis=0)
        fwin_ref[b] = window
        g = lax.dot_general(proj_ref[...], window, (((1,), (1,)), ((), ())), preferred_element_type=F32)
        g = 0.5 * g.astype(BF16).astype(F32)
        if b == 0:
            g = jnp.where(lane < HALO, OUTSIDE, g)
        if b == blocks - 1:
            g = jnp.where(lane >= HALO + bins, OUTSIDE, g)
        gwin_ref[b] = g.astype(BF16)
        dwin_ref[b] = jnp.zeros((ch, LANES), F32)

    head_col = column_ref[...]
    groups = bins // 8
    m_ref[:, : 2 * LANES] = jnp.zeros((48, 2 * LANES), BF16)
    m_ref[:, (groups + 2) * LANES :] = jnp.zeros((48, 2 * LANES), BF16)
    v_ref[...] = jnp.zeros(v_ref.shape, F32)
    inner = (lane1 >= HALO) & (lane1 < HALO + bins)

    def slot(s, x_acc):
        a, b, live = table_ref[0, s], table_ref[1, s], table_ref[2, s]
        weight = jnp.where(inner, live.astype(F32), 0.0)
        gr, gc = gwin_ref[a].astype(F32), gwin_ref[b].astype(F32)
        pred_r = jnp.sum(jnp.where(lane < HALO + bins, head_col * gr, 0.0), axis=0, keepdims=True)
        pred_c = jnp.sum(jnp.where(lane < HALO + bins, head_col * gc, 0.0), axis=0, keepdims=True)
        pred_r = jnp.transpose(jnp.broadcast_to(pred_r, (LANES, LANES)))

        def activations(g):
            for k in range(8):
                at = HALO - DIL + g * 8 + k
                x = gr[:, at : at + 1] + gc
                u_ref[k * ch : (k + 1) * ch, g * LANES : (g + 1) * LANES] = jnp.maximum(
                    x, 0.0
                ).astype(BF16)

        def misfit(c, z):
            terms = []
            for dx in range(3):
                tiles = [
                    z[c + dy][48 * dy + 24 * p + 8 * dx : 48 * dy + 24 * p + 8 * dx + 8]
                    for dy in range(3)
                    for p in range(2)
                ]
                while len(tiles) > 1:
                    tiles = [sum(tiles[i : i + 2]) for i in range(0, len(tiles), 2)]
                terms.append(tiles[0])
            conv = pltpu.roll(terms[0], DIL, 1) + terms[1] + pltpu.roll(terms[2], LANES - DIL, 1)
            goal = targets_ref[0, 0, s, c * 8 : (c + 1) * 8, :]
            goal = jnp.concatenate(
                [jnp.zeros((8, HALO), F32), goal, jnp.zeros((8, LANES - HALO - bins), F32)], axis=1
            )
            at = HALO + c * 8
            m = jnp.where(inner, (conv + pred_c + pred_r[at : at + 8] - goal) * weight, 0.0)
            moved = [pltpu.roll(m, LANES - DIL, 1), m, pltpu.roll(m, DIL, 1)]
            m_ref[:, (c + 2) * LANES : (c + 3) * LANES] = jnp.concatenate(
                moved + moved, axis=0
            ).astype(BF16)
            return m

        def gradients(g, d_rows, d_cols):
            cols = slice(g * LANES, (g + 2) * LANES)
            m3 = jnp.concatenate(
                [m_ref[:, (g + 2 - dy) * LANES : (g + 4 - dy) * LANES] for dy in range(3)], axis=0
            )
            up = jnp.dot(backward_ref[...], m3, preferred_element_type=F32)
            grad = jnp.where(u_ref[:, cols].astype(F32) > 0.0, up, 0.0)
            for k in range(16):
                at = slice(k // 8 * LANES, (k // 8 + 1) * LANES)
                part = grad[k % 8 * ch : (k % 8 + 1) * ch, at]
                d_cols = d_cols + part
                d_rows = jnp.where(
                    lane == HALO - DIL + g * 8 + k, jnp.sum(part, axis=1, keepdims=True), d_rows
                )
            return d_rows, d_cols

        z, m_cols, row_sums = [], jnp.zeros((8, LANES), F32), [jnp.zeros((HALO, LANES), F32)]
        d_rows = d_cols = jnp.zeros((ch, LANES), F32)
        def next_misfit(c, m_cols):
            m = misfit(c, z)
            row_sums.append(jnp.broadcast_to(jnp.sum(m, axis=1, keepdims=True), (8, LANES)))
            return m_cols + m

        def tap_sums(g):
            m3 = jnp.concatenate(
                [m_ref[:32, (g + 2 - dy) * LANES : (g + 4 - dy) * LANES] for dy in range(3)], axis=0
            )
            v_ref[...] += lax.dot_general(
                m3,
                u_ref[:, g * LANES : (g + 2) * LANES],
                (((1,), (1,)), ((), ())),
                preferred_element_type=F32,
            )

        for g in range(0, groups + 2, 2):
            activations(g)
            activations(g + 1)
            pair = jnp.dot(
                forward_ref[...],
                u_ref[:, g * LANES : (g + 2) * LANES],
                preferred_element_type=F32,
            )
            z += [pair[:, :LANES], pair[:, LANES:]]
        for c in range(groups // 2):
            m_cols = next_misfit(c, m_cols)
        for g in range(0, groups + 2, 2):
            d_rows, d_cols = gradients(g, d_rows, d_cols)
            tap_sums(g)
            for c in (groups // 2 + g, groups // 2 + g + 1):
                if c < groups:
                    m_cols = next_misfit(c, m_cols)
        row_sums.append(jnp.zeros((LANES - HALO - bins, LANES), F32))
        m_rows = jnp.transpose(jnp.concatenate(row_sums, axis=0))[:1]
        m_cols = jnp.sum(m_cols, axis=0, keepdims=True)
        d_rows = 0.5 * (d_rows + head_col * m_rows)
        d_cols = 0.5 * (d_cols + head_col * m_cols)
        dwin_ref[a] = dwin_ref[a] + d_rows
        dwin_ref[b] = dwin_ref[b] + d_cols
        return x_acc + jnp.where(m_rows != 0.0, gr * m_rows, 0.0) + jnp.where(
            m_cols != 0.0, gc * m_cols, 0.0
        )

    table_copy.wait()
    x_acc = lax.fori_loop(0, slots, slot, jnp.zeros((ch, LANES), F32))

    proj_acc = jnp.zeros((2 * ch, c1), F32)
    for b in range(blocks):
        hi, lo = split_two(dwin_ref[b])
        both = jnp.concatenate([hi, lo], axis=0).astype(BF16)
        proj_acc = proj_acc + jnp.dot(both, fwin_ref[b], preferred_element_type=F32)
    proj_acc = pad_to(proj_acc[:ch] + proj_acc[ch:], ch, LANES)

    wide = (96, 8 * ch)
    own_row = lax.broadcasted_iota(jnp.int32, wide, 0) % 8 == (
        lax.broadcasted_iota(jnp.int32, wide, 1) // ch
    )
    hi, lo = split_two(jnp.where(own_row, v_ref[...], 0.0))
    source = lax.broadcasted_iota(jnp.int32, (16, 96), 1)
    place = 3 * (source // 32) + source % 32 // 8
    select = (source % 32 < 24) & (lax.broadcasted_iota(jnp.int32, (16, 96), 0) == place)
    select = select.astype(F32).astype(BF16)
    v_rows = jnp.dot(select, hi.astype(BF16), preferred_element_type=F32) + jnp.dot(
        select, lo.astype(BF16), preferred_element_type=F32
    )
    v_sum = v_rows[:, :ch]
    for k in range(1, 8):
        v_sum = v_sum + v_rows[:, k * ch : (k + 1) * ch]
    sums = pltpu.roll(jnp.transpose(pad_to(v_sum, LANES, LANES))[:ch], 2 * ch, 1)
    sums = jnp.where(lane == 2 * ch + 9, jnp.sum(x_acc, axis=1, keepdims=True), sums)
    for r in range(rows_dev + 1):
        lower, upper = r, blocks - 1 - r
        keep_ref[r] = dwin_ref[jnp.where(odd, upper, lower)]
        give_ref[r] = dwin_ref[jnp.where(odd, lower, upper)]
    weights = jnp.where(lane < 2 * ch, proj_acc, sums)
    keep_ref[rows_dev + 1] = weights
    give_ref[rows_dev + 1] = weights


def pair_kernel(keep_ref, took_ref, out_ref):
    bands, ch = keep_ref.shape[0] - 2, keep_ref.shape[1]
    odd = lax.axis_index("col") % 2 == 1
    bins = LANES // 2
    cols_dev = out_ref.shape[0] // bands
    part = bins // cols_dev
    weights = keep_ref[bands + 1] + took_ref[bands + 1]
    chunks = [weights[16 * q : 16 * q + 16] for q in range(3)]
    lane16 = lane_iota(16)

    def share(dest, k):
        first = 48 * dest + 24 * k
        moved = [pltpu.roll(chunks[q], (48 + 24 * q - first) % LANES, 1) for q in range(3)]
        v_own = pltpu.roll(chunks[2 * k], 24 - 5 * dest, 1)
        v_middle = pltpu.roll(chunks[1], 29 - 5 * dest - 3 * k, 1)
        out = jnp.where(lane16 < 125, v_own, v_middle)
        for q in (2, 1, 0):
            out = jnp.where(lane16 < 72 + 24 * q, moved[q], out)
        return out

    shares = [jnp.where(odd, share(dest, 1), share(dest, 0)) for dest in range(2)]
    lane_part = lane_iota(part)
    windows = [
        jnp.transpose(pad_to(keep_ref[r] + took_ref[r], LANES, LANES)) for r in range(bands + 1)
    ]
    first, end = HALO, HALO + bins
    for r in range(bands):
        after = windows[r + 1]
        before = windows[r - 1] if r > 0 else jnp.zeros((LANES, LANES), F32)
        at_start = jnp.where(odd, after[end : end + DIL], before[end : end + DIL])
        at_end = jnp.where(odd, before[first - DIL : first], after[first - DIL : first])
        own = windows[r]
        block = jnp.concatenate(
            [
                own[first : first + DIL] + at_start,
                own[first + DIL : end - DIL],
                own[end - DIL : end] + at_end,
            ],
            axis=0,
        )
        for c in range(cols_dev):
            dest = r * cols_dev + c
            base = shares[c % 2]
            rows = block[c * part : (c + 1) * part]
            out_ref[dest, :part] = jnp.where(lane_part < ch, rows, base[:part]).astype(BF16)
            if part < 16:
                out_ref[dest, part:] = base[part:].astype(BF16)


def total_kernel(got_ref, total_ref):
    totals = [got_ref[d].astype(F32) for d in range(4)]
    for d in range(4, got_ref.shape[0]):
        totals[d % 4] = totals[d % 4] + got_ref[d].astype(F32)
    total_ref[:16] = totals[0] + totals[2]
    total_ref[16:] = totals[1] + totals[3]


def features_kernel(root, total_ref, proj_ref, feat_ref):
    ch = proj_ref.shape[0]
    part = feat_ref.shape[2]
    rows = [total_ref[16 * half : 16 * half + part, :ch] for half in range(2)]
    hi, lo = split_two(jnp.concatenate(rows, axis=0))
    feat = jnp.dot(
        jnp.concatenate([hi, lo], axis=0).astype(BF16), proj_ref[...], preferred_element_type=F32
    )
    for half in range(2):
        at = half * part
        feat_ref[0, half] = (feat[at : at + part] + feat[2 * part + at : 3 * part + at]) * root


def weights_kernel(scale, mine_ref, other_ref, conv_ref, column_ref, proj_out_ref, conv_out_ref, head_out_ref):
    ch = conv_ref.shape[1]
    odd = lax.axis_index("col") % 2 == 1
    mine, other = mine_ref[...], other_ref[...]
    lane16 = lane_iota(16)
    parts = (jnp.where(odd, other, mine), jnp.where(odd, mine, other))

    def sent(dest, k, shift):
        return pltpu.roll(parts[dest][16 * k : 16 * k + 16], shift % LANES, 1)

    proj_rows = []
    for q in range(3):
        rows = sent(1, 1, 72 - 48 - 24 * q)
        for n in (2, 1, 0):
            rows = jnp.where(lane16 < 24 * n + 24, sent(n // 2, n % 2, 24 * n - 48 - 24 * q), rows)
        proj_rows.append(rows)
    proj_out_ref[...] = jnp.concatenate(proj_rows, axis=0)[:, : 2 * ch] * scale
    v_rows = []
    for q in range(3):
        by_dest = []
        for dest in range(2):
            if q == 1:
                first, second = sent(dest, 0, 5 * dest - 125), sent(dest, 1, 5 * dest + 3 - 125)
                by_dest.append(jnp.where(lane16 < 5 * dest + 3, first, second))
            else:
                by_dest.append(sent(dest, q // 2, 5 * dest - 120))
        v_rows.append(jnp.where(lane16 < 5, by_dest[0], by_dest[1]))
    sums = jnp.concatenate(v_rows, axis=0)
    sums = jnp.transpose(pad_to(sums, LANES, LANES))[:10, :ch]
    head_col = column_ref[:, :ch] * scale
    products = jnp.zeros((ch, ch), F32)
    for t in range(9):
        v = sums[t : t + 1]
        conv_out_ref[t] = head_col * v
        products = products + conv_ref[t].astype(F32) * v
    head_sum = jnp.sum(jnp.transpose(pad_to(products, LANES, LANES)), axis=0, keepdims=True)[:, :ch]
    head_out_ref[...] = (sums[9:10] + head_sum) * scale


def body(feats, proj_weight, conv_weight, head_weight, tile_table, targets):
    rows_dev, cols_dev = lax.axis_size("row"), lax.axis_size("col")
    devices = rows_dev * cols_dev
    _, halves, part, c1 = feats.shape
    ch = proj_weight.shape[1]
    proj_t, conv_t = proj_weight.T, conv_weight.transpose(1, 0, 2)
    bins = part * cols_dev
    blocks = halves * rows_dev
    sequence_length = blocks * bins
    slots = tile_table.shape[2]
    scale = 1.0 / (sequence_length * bins)

    mine = lax.all_to_all(
        jnp.broadcast_to(feats, (devices // halves,) + feats.shape[1:]).reshape(devices, part, c1),
        ("row", "col"),
        0,
        0,
        tiled=True,
    )
    cores = [(c, c ^ 1) for c in range(cols_dev)]
    other = lax.ppermute(mine, "col", cores)
    if part % 16:
        mine, other = mine.reshape(rows_dev, bins, c1), other.reshape(rows_dev, bins, c1)
    vmem = pl.BlockSpec(memory_space=pltpu.VMEM)
    params = pltpu.CompilerParams(vmem_limit_bytes=48 * 1024 * 1024)
    forward, backward, head_column, entries = pl.pallas_call(
        taps_kernel,
        out_shape=(
            jax.ShapeDtypeStruct((144, 8 * ch), BF16),
            jax.ShapeDtypeStruct((8 * ch, 144), BF16),
            jax.ShapeDtypeStruct((ch, LANES), F32),
            jax.ShapeDtypeStruct((8, LANES), jnp.int32),
        ),
        in_specs=[vmem, vmem, vmem],
        out_specs=(vmem, vmem, vmem, vmem),
        compiler_params=params,
        cost_estimate=pl.CostEstimate(flops=10**7, bytes_accessed=10**6, transcendentals=0),
        name="taps",
    )(conv_t, head_weight.reshape(1, ch), tile_table.transpose(0, 3, 1, 2))
    keep, give = pl.pallas_call(
        functools.partial(tiles_kernel, rows_dev, slots),
        out_shape=(jax.ShapeDtypeStruct((rows_dev + 2, ch, LANES), F32),) * 2,
        in_specs=[vmem] * 8,
        out_specs=(vmem, vmem),
        scratch_shapes=[
            pltpu.VMEM((blocks, LANES, c1), BF16),
            pltpu.VMEM((blocks, ch, LANES), BF16),
            pltpu.VMEM((blocks, ch, LANES), F32),
            pltpu.VMEM((8 * ch, (bins // 8 + 2) * LANES), BF16),
            pltpu.VMEM((48, (bins // 8 + 4) * LANES), BF16),
            pltpu.VMEM((96, 8 * ch), F32),
            pltpu.SMEM((8, LANES), jnp.int32),
            pltpu.SemaphoreType.DMA,
        ],
        compiler_params=params,
        name="tiles",
    )(mine, other, proj_t, forward, backward, head_column, entries, targets)
    took = lax.ppermute(give, "col", cores)
    partial = pl.pallas_call(
        pair_kernel,
        out_shape=jax.ShapeDtypeStruct((devices, 16, LANES), BF16),
        in_specs=[vmem, vmem],
        out_specs=vmem,
        compiler_params=params,
        name="pair",
    )(keep, took)
    got = lax.all_to_all(partial, ("row", "col"), 0, 0, tiled=True)
    own_total = pl.pallas_call(
        total_kernel,
        out_shape=jax.ShapeDtypeStruct((32, LANES), F32),
        in_specs=[vmem],
        out_specs=vmem,
        compiler_params=params,
        name="total",
    )(got)
    other_total = lax.ppermute(own_total, "col", cores)
    feat_grad = pl.pallas_call(
        functools.partial(features_kernel, 1.0 / math.sqrt(sequence_length)),
        out_shape=jax.ShapeDtypeStruct(feats.shape, F32),
        in_specs=[vmem, vmem],
        out_specs=vmem,
        compiler_params=params,
        cost_estimate=pl.CostEstimate(flops=10**7, bytes_accessed=10**6, transcendentals=0),
        name="features",
    )(own_total, proj_t)
    proj_grad, conv_grad, head_grad = pl.pallas_call(
        functools.partial(weights_kernel, scale),
        out_shape=(
            jax.ShapeDtypeStruct(proj_t.shape, F32),
            jax.ShapeDtypeStruct(conv_t.shape, F32),
            jax.ShapeDtypeStruct((1, ch), F32),
        ),
        in_specs=[vmem, vmem, vmem, vmem],
        out_specs=(vmem, vmem, vmem),
        compiler_params=params,
        name="weights",
    )(own_total, other_total, conv_t, head_column)
    return feat_grad, proj_grad.T, conv_grad.transpose(1, 0, 2), head_grad.reshape(ch)


def solution(mesh):
    return jax.shard_map(
        body,
        mesh=mesh,
        in_specs=(
            P("row", None, "col", None),
            P(),
            P(),
            P(),
            P("row", "col", None, None),
            P("row", "col", None, None, None),
        ),
        out_specs=(P("row", None, "col", None), P(), P(), P()),
        check_vma=False,
    )
```

```python
import functools
import math

import jax
import jax.numpy as jnp
from jax import lax
from jax.experimental import pallas as pl
from jax.experimental.pallas import tpu as pltpu
from jax.sharding import PartitionSpec as P

DIL = 8
LANES = 128
HALO = 16
F32 = jnp.float32
BF16 = jnp.bfloat16
FIELD = 32
OUTSIDE = -1e30


def lane_iota(rows):
    return lax.broadcasted_iota(jnp.int32, (rows, LANES), 1)


def split_two(x):
    high = x.astype(BF16).astype(F32)
    return high, x - high


def pad_to(x, rows, cols):
    r, c = x.shape
    if c < cols:
        x = jnp.concatenate([x, jnp.zeros((r, cols - c), x.dtype)], axis=1)
    if r < rows:
        x = jnp.concatenate([x, jnp.zeros((rows - r, cols), x.dtype)], axis=0)
    return x


def taps_kernel(conv_ref, head_ref, table_ref, forward_ref, backward_ref, column_ref, entries_ref):
    ch = conv_ref.shape[1]
    table = pad_to(table_ref[0, :, 0, :], 8, LANES)
    row = table[:1]
    for k in (1, 2):
        row = row + pltpu.roll(table[k : k + 1], FIELD * k, 1)
    entries_ref[...] = row
    head_col = jnp.transpose(jnp.broadcast_to(pad_to(head_ref[...], 1, LANES), (LANES, LANES)))[:ch]
    taps = [
        jnp.sum(head_col[:, :ch] * conv_ref[t].astype(F32), axis=0, keepdims=True)
        for t in range(9)
    ]
    wide = (8, 8 * ch)
    diagonal = lax.broadcasted_iota(jnp.int32, wide, 1) // ch == lax.broadcasted_iota(
        jnp.int32, wide, 0
    )
    hi_tiles, lo_tiles = [
        [
            jnp.where(diagonal, jnp.broadcast_to(jnp.concatenate([row] * 8, axis=1), wide), 0.0)
            for row in rows
        ]
        for rows in zip(*[split_two(row) for row in taps])
    ]
    forward_rows, backward_rows = [], []
    for dy in range(3):
        hi, lo = hi_tiles[3 * dy : 3 * dy + 3], lo_tiles[3 * dy : 3 * dy + 3]
        forward_rows += hi + lo
        backward_rows += hi + lo
    forward_taps = jnp.concatenate(forward_rows, axis=0).astype(BF16)
    pad = [jnp.zeros((112, 8 * ch), F32)]
    backward_taps = jnp.transpose(jnp.concatenate(backward_rows + pad, axis=0))[:, :144].astype(BF16)
    forward_ref[...] = forward_taps
    backward_ref[...] = backward_taps
    column_ref[...] = head_col


def tiles_kernel(
    rows_dev,
    slots,
    mine_ref,
    other_ref,
    proj_ref,
    forward_ref,
    backward_ref,
    column_ref,
    entries_ref,
    targets_ref,
    keep_ref,
    give_ref,
    fwin_ref,
    gwin_ref,
    dwin_ref,
    u_ref,
    m_ref,
    v_ref,
    table_ref,
    table_sem,
):
    table_copy = pltpu.make_async_copy(entries_ref, table_ref, table_sem)
    table_copy.start()
    n_src, chunk, c1 = mine_ref.shape
    odd = lax.axis_index("col") % 2 == 1
    cols_dev = n_src // rows_dev
    blocks = 2 * rows_dev
    bins = cols_dev * chunk
    ch = proj_ref.shape[0]
    lane = lane_iota(ch)
    lane1 = lane_iota(1)

    def chunks_of(b):
        r, half = (b, 0) if b < rows_dev else (blocks - 1 - b, 1)
        first, second = (mine_ref, other_ref) if half == 0 else (other_ref, mine_ref)
        return [
            jnp.where(odd, second[r * cols_dev + c], first[r * cols_dev + c])
            for c in range(cols_dev)
        ]

    zero_halo = jnp.zeros((HALO, c1), BF16)
    for b in range(blocks):
        before = chunks_of(b - 1)[-1][chunk - HALO :] if b > 0 else zero_halo
        after = chunks_of(b + 1)[0][:HALO] if b < blocks - 1 else zero_halo
        tail = jnp.zeros((LANES - bins - 2 * HALO, c1), BF16)
        window = jnp.concatenate([before] + chunks_of(b) + [after, tail], axis=0)
        fwin_ref[b] = window
        g = lax.dot_general(proj_ref[...], window, (((1,), (1,)), ((), ())), preferred_element_type=F32)
        g = 0.5 * g.astype(BF16).astype(F32)
        if b == 0:
            g = jnp.where(lane < HALO, OUTSIDE, g)
        if b == blocks - 1:
            g = jnp.where(lane >= HALO + bins, OUTSIDE, g)
        gwin_ref[b] = g.astype(BF16)
        dwin_ref[b] = jnp.zeros((ch, LANES), F32)

    head_col = column_ref[...]
    groups = bins // 8
    m_ref[:, : 2 * LANES] = jnp.zeros((48, 2 * LANES), BF16)
    m_ref[:, (groups + 2) * LANES :] = jnp.zeros((48, 2 * LANES), BF16)
    v_ref[...] = jnp.zeros(v_ref.shape, F32)
    inner = (lane1 >= HALO) & (lane1 < HALO + bins)

    def slot(s, x_acc):
        a, b, live = table_ref[0, FIELD * 0 + s], table_ref[0, FIELD * 1 + s], table_ref[0, FIELD * 2 + s]
        weight = jnp.where(inner, live.astype(F32), 0.0)
        gr, gc = gwin_ref[a].astype(F32), gwin_ref[b].astype(F32)
        pred_r = jnp.sum(jnp.where(lane < HALO + bins, head_col * gr, 0.0), axis=0, keepdims=True)
        pred_c = jnp.sum(jnp.where(lane < HALO + bins, head_col * gc, 0.0), axis=0, keepdims=True)
        pred_r = jnp.transpose(jnp.broadcast_to(pred_r, (LANES, LANES)))

        def activations(g):
            for k in range(8):
                at = HALO - DIL + g * 8 + k
                x = gr[:, at : at + 1] + gc
                u_ref[k * ch : (k + 1) * ch, g * LANES : (g + 1) * LANES] = jnp.maximum(
                    x, 0.0
                ).astype(BF16)

        def misfit(c, z):
            terms = []
            for dx in range(3):
                tiles = [
                    z[c + dy][48 * dy + 24 * p + 8 * dx : 48 * dy + 24 * p + 8 * dx + 8]
                    for dy in range(3)
                    for p in range(2)
                ]
                while len(tiles) > 1:
                    tiles = [sum(tiles[i : i + 2]) for i in range(0, len(tiles), 2)]
                terms.append(tiles[0])
            conv = pltpu.roll(terms[0], DIL, 1) + terms[1] + pltpu.roll(terms[2], LANES - DIL, 1)
            goal = targets_ref[0, 0, s, c * 8 : (c + 1) * 8, :]
            goal = jnp.concatenate(
                [jnp.zeros((8, HALO), F32), goal, jnp.zeros((8, LANES - HALO - bins), F32)], axis=1
            )
            at = HALO + c * 8
            m = jnp.where(inner, (conv + pred_c + pred_r[at : at + 8] - goal) * weight, 0.0)
            moved = [pltpu.roll(m, LANES - DIL, 1), m, pltpu.roll(m, DIL, 1)]
            m_ref[:, (c + 2) * LANES : (c + 3) * LANES] = jnp.concatenate(
                moved + moved, axis=0
            ).astype(BF16)
            return m

        def gradients(g, d_rows, d_cols):
            cols = slice(g * LANES, (g + 2) * LANES)
            m3 = jnp.concatenate(
                [m_ref[:, (g + 2 - dy) * LANES : (g + 4 - dy) * LANES] for dy in range(3)], axis=0
            )
            up = jnp.dot(backward_ref[...], m3, preferred_element_type=F32)
            grad = jnp.where(u_ref[:, cols].astype(F32) > 0.0, up, 0.0)
            for k in range(16):
                at = slice(k // 8 * LANES, (k // 8 + 1) * LANES)
                part = grad[k % 8 * ch : (k % 8 + 1) * ch, at]
                d_cols = d_cols + part
                d_rows = jnp.where(
                    lane == HALO - DIL + g * 8 + k, jnp.sum(part, axis=1, keepdims=True), d_rows
                )
            return d_rows, d_cols

        z, m_cols, row_sums = [], jnp.zeros((8, LANES), F32), [jnp.zeros((HALO, LANES), F32)]
        d_rows = d_cols = jnp.zeros((ch, LANES), F32)
        def next_misfit(c, m_cols):
            m = misfit(c, z)
            row_sums.append(jnp.broadcast_to(jnp.sum(m, axis=1, keepdims=True), (8, LANES)))
            return m_cols + m

        def tap_sums(g):
            m3 = jnp.concatenate(
                [m_ref[:32, (g + 2 - dy) * LANES : (g + 4 - dy) * LANES] for dy in range(3)], axis=0
            )
            v_ref[...] += lax.dot_general(
                m3,
                u_ref[:, g * LANES : (g + 2) * LANES],
                (((1,), (1,)), ((), ())),
                preferred_element_type=F32,
            )

        activations(0)
        activations(1)
        for g in range(0, groups + 2, 2):
            if g + 2 < groups + 2:
                activations(g + 2)
                activations(g + 3)
            pair = jnp.dot(
                forward_ref[...],
                u_ref[:, g * LANES : (g + 2) * LANES],
                preferred_element_type=F32,
            )
            z += [pair[:, :LANES], pair[:, LANES:]]
        for c in range(groups // 2):
            m_cols = next_misfit(c, m_cols)
        for g in range(0, groups + 2, 2):
            d_rows, d_cols = gradients(g, d_rows, d_cols)
            if g >= 4:
                tap_sums(g - 4)
            for c in (groups // 2 + g, groups // 2 + g + 1):
                if c < groups:
                    m_cols = next_misfit(c, m_cols)
        for g in (groups - 2, groups):
            tap_sums(g)
        row_sums.append(jnp.zeros((LANES - HALO - bins, LANES), F32))
        m_rows = jnp.transpose(jnp.concatenate(row_sums, axis=0))[:1]
        m_cols = jnp.sum(m_cols, axis=0, keepdims=True)
        d_rows = 0.5 * (d_rows + head_col * m_rows)
        d_cols = 0.5 * (d_cols + head_col * m_cols)
        dwin_ref[a] = dwin_ref[a] + d_rows
        dwin_ref[b] = dwin_ref[b] + d_cols
        return x_acc + jnp.where(m_rows != 0.0, gr * m_rows, 0.0) + jnp.where(
            m_cols != 0.0, gc * m_cols, 0.0
        )

    table_copy.wait()
    x_acc = lax.fori_loop(0, slots, slot, jnp.zeros((ch, LANES), F32))

    proj_acc = jnp.zeros((2 * ch, c1), F32)
    for b in range(blocks):
        hi, lo = split_two(dwin_ref[b])
        both = jnp.concatenate([hi, lo], axis=0).astype(BF16)
        proj_acc = proj_acc + jnp.dot(both, fwin_ref[b], preferred_element_type=F32)
    proj_acc = pad_to(proj_acc[:ch] + proj_acc[ch:], ch, LANES)

    wide = (96, 8 * ch)
    own_row = lax.broadcasted_iota(jnp.int32, wide, 0) % 8 == (
        lax.broadcasted_iota(jnp.int32, wide, 1) // ch
    )
    hi, lo = split_two(jnp.where(own_row, v_ref[...], 0.0))
    source = lax.broadcasted_iota(jnp.int32, (16, 96), 1)
    place = 3 * (source // 32) + source % 32 // 8
    select = (source % 32 < 24) & (lax.broadcasted_iota(jnp.int32, (16, 96), 0) == place)
    select = select.astype(F32).astype(BF16)
    v_rows = jnp.dot(select, hi.astype(BF16), preferred_element_type=F32) + jnp.dot(
        select, lo.astype(BF16), preferred_element_type=F32
    )
    v_sum = v_rows[:, :ch]
    for k in range(1, 8):
        v_sum = v_sum + v_rows[:, k * ch : (k + 1) * ch]
    sums = pltpu.roll(jnp.transpose(pad_to(v_sum, LANES, LANES))[:ch], 2 * ch, 1)
    sums = jnp.where(lane == 2 * ch + 9, jnp.sum(x_acc, axis=1, keepdims=True), sums)
    for r in range(rows_dev + 1):
        lower, upper = r, blocks - 1 - r
        keep_ref[r] = dwin_ref[jnp.where(odd, upper, lower)]
        give_ref[r] = dwin_ref[jnp.where(odd, lower, upper)].astype(BF16)
    weights = jnp.where(lane < 2 * ch, proj_acc, sums)
    keep_ref[rows_dev + 1] = weights
    give_ref[rows_dev + 1] = weights.astype(BF16)


def pair_kernel(keep_ref, took_ref, out_ref):
    bands, ch = keep_ref.shape[0] - 2, keep_ref.shape[1]
    odd = lax.axis_index("col") % 2 == 1
    bins = LANES // 2
    cols_dev = out_ref.shape[0] // bands
    part = bins // cols_dev
    weights = keep_ref[bands + 1] + took_ref[bands + 1].astype(F32)
    chunks = [weights[16 * q : 16 * q + 16] for q in range(3)]
    lane16 = lane_iota(16)

    def share(dest, k):
        first = 48 * dest + 24 * k
        moved = [pltpu.roll(chunks[q], (48 + 24 * q - first) % LANES, 1) for q in range(3)]
        v_own = pltpu.roll(chunks[2 * k], 24 - 5 * dest, 1)
        v_middle = pltpu.roll(chunks[1], 29 - 5 * dest - 3 * k, 1)
        out = jnp.where(lane16 < 125, v_own, v_middle)
        for q in (2, 1, 0):
            out = jnp.where(lane16 < 72 + 24 * q, moved[q], out)
        return out

    shares = [jnp.where(odd, share(dest, 1), share(dest, 0)) for dest in range(2)]
    lane_part = lane_iota(part)
    windows = [
        jnp.transpose(pad_to(keep_ref[r] + took_ref[r].astype(F32), LANES, LANES))
        for r in range(bands + 1)
    ]
    first, end = HALO, HALO + bins
    for r in range(bands):
        after = windows[r + 1]
        before = windows[r - 1] if r > 0 else jnp.zeros((LANES, LANES), F32)
        at_start = jnp.where(odd, after[end : end + DIL], before[end : end + DIL])
        at_end = jnp.where(odd, before[first - DIL : first], after[first - DIL : first])
        own = windows[r]
        block = jnp.concatenate(
            [
                own[first : first + DIL] + at_start,
                own[first + DIL : end - DIL],
                own[end - DIL : end] + at_end,
            ],
            axis=0,
        )
        for c in range(cols_dev):
            dest = r * cols_dev + c
            base = shares[c % 2]
            rows = block[c * part : (c + 1) * part]
            out_ref[dest, :part] = jnp.where(lane_part < ch, rows, base[:part]).astype(BF16)
            if part < 16:
                out_ref[dest, part:] = base[part:].astype(BF16)


def total_kernel(got_ref, total_ref):
    totals = [got_ref[d].astype(F32) for d in range(4)]
    for d in range(4, got_ref.shape[0]):
        totals[d % 4] = totals[d % 4] + got_ref[d].astype(F32)
    total_ref[:16] = totals[0] + totals[2]
    total_ref[16:] = totals[1] + totals[3]


def features_kernel(root, total_ref, proj_ref, feat_ref):
    ch = proj_ref.shape[0]
    part = feat_ref.shape[2]
    rows = [total_ref[16 * half : 16 * half + part, :ch] for half in range(2)]
    hi, lo = split_two(jnp.concatenate(rows, axis=0))
    feat = jnp.dot(
        jnp.concatenate([hi, lo], axis=0).astype(BF16), proj_ref[...], preferred_element_type=F32
    )
    for half in range(2):
        at = half * part
        feat_ref[0, half] = (feat[at : at + part] + feat[2 * part + at : 3 * part + at]) * root


def weights_kernel(scale, mine_ref, other_ref, conv_ref, column_ref, proj_out_ref, conv_out_ref, head_out_ref):
    ch = conv_ref.shape[1]
    odd = lax.axis_index("col") % 2 == 1
    mine, other = mine_ref[...], other_ref[...]
    lane16 = lane_iota(16)
    parts = (jnp.where(odd, other, mine), jnp.where(odd, mine, other))

    def sent(dest, k, shift):
        return pltpu.roll(parts[dest][16 * k : 16 * k + 16], shift % LANES, 1)

    proj_rows = []
    for q in range(3):
        rows = sent(1, 1, 72 - 48 - 24 * q)
        for n in (2, 1, 0):
            rows = jnp.where(lane16 < 24 * n + 24, sent(n // 2, n % 2, 24 * n - 48 - 24 * q), rows)
        proj_rows.append(rows)
    proj_out_ref[...] = jnp.concatenate(proj_rows, axis=0)[:, : 2 * ch] * scale
    v_rows = []
    for q in range(3):
        by_dest = []
        for dest in range(2):
            if q == 1:
                first, second = sent(dest, 0, 5 * dest - 125), sent(dest, 1, 5 * dest + 3 - 125)
                by_dest.append(jnp.where(lane16 < 5 * dest + 3, first, second))
            else:
                by_dest.append(sent(dest, q // 2, 5 * dest - 120))
        v_rows.append(jnp.where(lane16 < 5, by_dest[0], by_dest[1]))
    sums = jnp.concatenate(v_rows, axis=0)
    sums = jnp.transpose(pad_to(sums, LANES, LANES))[:10, :ch]
    head_col = column_ref[:, :ch] * scale
    products = jnp.zeros((ch, ch), F32)
    for t in range(9):
        v = sums[t : t + 1]
        conv_out_ref[t] = head_col * v
        products = products + conv_ref[t].astype(F32) * v
    head_sum = jnp.sum(jnp.transpose(pad_to(products, LANES, LANES)), axis=0, keepdims=True)[:, :ch]
    head_out_ref[...] = (sums[9:10] + head_sum) * scale


def body(feats, proj_weight, conv_weight, head_weight, tile_table, targets):
    rows_dev, cols_dev = lax.axis_size("row"), lax.axis_size("col")
    devices = rows_dev * cols_dev
    _, halves, part, c1 = feats.shape
    ch = proj_weight.shape[1]
    proj_t, conv_t = proj_weight.T, conv_weight.transpose(1, 0, 2)
    bins = part * cols_dev
    blocks = halves * rows_dev
    sequence_length = blocks * bins
    slots = tile_table.shape[2]
    scale = 1.0 / (sequence_length * bins)

    mine = lax.all_to_all(
        jnp.broadcast_to(feats, (devices // halves,) + feats.shape[1:]).reshape(devices, part, c1),
        ("row", "col"),
        0,
        0,
        tiled=True,
    )
    cores = [(c, c ^ 1) for c in range(cols_dev)]
    other = lax.ppermute(mine, "col", cores)
    if part % 16:
        mine, other = mine.reshape(rows_dev, bins, c1), other.reshape(rows_dev, bins, c1)
    vmem = pl.BlockSpec(memory_space=pltpu.VMEM)
    params = pltpu.CompilerParams(vmem_limit_bytes=48 * 1024 * 1024)
    forward, backward, head_column, entries = pl.pallas_call(
        taps_kernel,
        out_shape=(
            jax.ShapeDtypeStruct((144, 8 * ch), BF16),
            jax.ShapeDtypeStruct((8 * ch, 144), BF16),
            jax.ShapeDtypeStruct((ch, LANES), F32),
            jax.ShapeDtypeStruct((1, LANES), jnp.int32),
        ),
        in_specs=[vmem, vmem, vmem],
        out_specs=(vmem, vmem, vmem, vmem),
        compiler_params=params,
        cost_estimate=pl.CostEstimate(flops=10**7, bytes_accessed=10**6, transcendentals=0),
        name="taps",
    )(conv_t, head_weight.reshape(1, ch), tile_table.transpose(0, 3, 1, 2))
    keep, give = pl.pallas_call(
        functools.partial(tiles_kernel, rows_dev, slots),
        out_shape=tuple(
            jax.ShapeDtypeStruct((rows_dev + 2, ch, LANES), dtype) for dtype in (F32, BF16)
        ),
        in_specs=[vmem] * 8,
        out_specs=(vmem, vmem),
        scratch_shapes=[
            pltpu.VMEM((blocks, LANES, c1), BF16),
            pltpu.VMEM((blocks, ch, LANES), BF16),
            pltpu.VMEM((blocks, ch, LANES), F32),
            pltpu.VMEM((8 * ch, (bins // 8 + 2) * LANES), BF16),
            pltpu.VMEM((48, (bins // 8 + 4) * LANES), BF16),
            pltpu.VMEM((96, 8 * ch), F32),
            pltpu.SMEM((1, LANES), jnp.int32),
            pltpu.SemaphoreType.DMA,
        ],
        compiler_params=params,
        name="tiles",
    )(mine, other, proj_t, forward, backward, head_column, entries, targets)
    took = lax.ppermute(give, "col", cores)
    partial = pl.pallas_call(
        pair_kernel,
        out_shape=jax.ShapeDtypeStruct((devices, 16, LANES), BF16),
        in_specs=[vmem, vmem],
        out_specs=vmem,
        compiler_params=params,
        name="pair",
    )(keep, took)
    got = lax.all_to_all(partial, ("row", "col"), 0, 0, tiled=True)
    own_total = pl.pallas_call(
        total_kernel,
        out_shape=jax.ShapeDtypeStruct((32, LANES), F32),
        in_specs=[vmem],
        out_specs=vmem,
        compiler_params=params,
        name="total",
    )(got)
    other_total = lax.ppermute(own_total, "col", cores)
    feat_grad = pl.pallas_call(
        functools.partial(features_kernel, 1.0 / math.sqrt(sequence_length)),
        out_shape=jax.ShapeDtypeStruct(feats.shape, F32),
        in_specs=[vmem, vmem],
        out_specs=vmem,
        compiler_params=params,
        cost_estimate=pl.CostEstimate(flops=10**7, bytes_accessed=10**6, transcendentals=0),
        name="features",
    )(own_total, proj_t)
    proj_grad, conv_grad, head_grad = pl.pallas_call(
        functools.partial(weights_kernel, scale),
        out_shape=(
            jax.ShapeDtypeStruct(proj_t.shape, F32),
            jax.ShapeDtypeStruct(conv_t.shape, F32),
            jax.ShapeDtypeStruct((1, ch), F32),
        ),
        in_specs=[vmem, vmem, vmem, vmem],
        out_specs=(vmem, vmem, vmem),
        compiler_params=params,
        name="weights",
    )(own_total, other_total, conv_t, head_column)
    return feat_grad, proj_grad.T, conv_grad.transpose(1, 0, 2), head_grad.reshape(ch)


def solution(mesh):
    return jax.shard_map(
        body,
        mesh=mesh,
        in_specs=(
            P("row", None, "col", None),
            P(),
            P(),
            P(),
            P("row", "col", None, None),
            P("row", "col", None, None, None),
        ),
        out_specs=(P("row", None, "col", None), P(), P(), P()),
        check_vma=False,
    )
```
